32 devices in a mesh: ctx: 16 (over z, y, x), tp: 2 (over core).
Axes of the slice: x: 2, y: 2, z: 4, core: 2. Of those that a mesh axis runs over, the one named last changes fastest.
Arguments:
- signal: float32 [4096, 2048], P('tp', 'ctx'), may hold values from -0.03125 to 0.03125
- cotangent: float32 [4096, 2048], P('tp', 'ctx'), may hold values from -6 to 6
- filters: float32 [256, 2048], P(None, 'ctx'), may hold values from -0.125 to 0.125
Outputs:
- grad_signal: float32 [4096, 2048], P('tp', 'ctx')
- grad_filters: float32 [256, 2048], P(None, 'ctx')
The draws below stay inside these ranges and needn't reach their ends.
All inputs are finite; a program needn't handle non-finite values.
Results may differ from the reference program's by a relative error of at most 0.0001.
Values sent between devices are 32-bit elements; how exact they have to be, the bound alone decides.
No kernel may reach another device: no remote copies, remote signals or barrier semaphores. Data moves between devices by JAX's collectives and lax.ppermute only.
A program may use at most 128 MiB of HBM per device.

```python
import jax
import jax.numpy as jnp
from jax import lax

CHANNELS = 4096
FILTERS = 256
GROUP = 16
LEN = 2048


def levels(stream_key, extent, shards, least, largest):
    factor_of = 1.0
    for axis_at, blocks in shards:
        heights = jax.random.uniform(jax.random.fold_in(jax.random.fold_in(stream_key, 6), axis_at), (blocks,), jnp.float32, least / len(shards), largest / len(shards))
        factor_of = factor_of * jnp.repeat(jnp.exp(heights), extent[axis_at] // blocks).reshape((-1,) + (1,) * (len(extent) - 1 - axis_at))
    return factor_of


def bell_draw(own_key, dims, deviation, reach, cuts=(), held_as=jnp.bfloat16):
    array = jax.random.normal(own_key, dims, jnp.float32) * deviation
    if len(cuts) > 0:
        array = levels(own_key, dims, cuts, -0.22, 0.18) * array
    return jnp.clip(array, min=-reach, max=reach).astype(held_as)


def setup_inputs(seed: int = 0) -> dict:
    streams_of = jax.random.split(jax.random.key(seed), 4)
    return {
        "signal": bell_draw(streams_of[0], (CHANNELS, LEN), (GROUP * LEN) ** -0.5, 0.03125, ((0, 2), (1, 16)), jnp.float32),
        "cotangent": bell_draw(streams_of[1], (CHANNELS, LEN), 1.0, 6.0, ((0, 2), (1, 16)), jnp.float32),
        "filters": bell_draw(streams_of[2], (FILTERS, LEN), LEN ** -0.5, 0.125, ((1, 16),), jnp.float32),
    }


def reference(signal, cotangent, filters):
    total = 2 * LEN
    spec_fil = jnp.fft.rfft(filters, n=total, axis=1)
    sig_groups = signal.reshape(GROUP, FILTERS, LEN)
    cot_groups = cotangent.reshape(GROUP, FILTERS, LEN)

    def one_group(carry, pieces):
        sig_piece, cot_piece = pieces
        spec_sig = jnp.fft.rfft(sig_piece, n=total, axis=1)
        spec_cot = jnp.fft.rfft(cot_piece, n=total, axis=1)
        grad_piece = jnp.fft.irfft(jnp.conj(spec_fil) * spec_cot, n=total, axis=1)[:, :LEN]
        return carry + jnp.conj(spec_sig) * spec_cot, grad_piece

    grouped, grad_pieces = lax.scan(one_group, jnp.zeros_like(spec_fil), (sig_groups, cot_groups))
    grad_signal = grad_pieces.reshape(CHANNELS, LEN)
    grad_filters = jnp.fft.irfft(grouped, n=total, axis=1)[:, :LEN]
    return grad_signal.astype(signal.dtype), grad_filters.astype(signal.dtype)
```

```python
import functools

import jax
import jax.numpy as jnp
from jax import lax
from jax.experimental import pallas as pl
from jax.experimental.pallas import tpu as pltpu
from jax.sharding import PartitionSpec as P

f32, bf16 = jnp.float32, jnp.bfloat16
PAIR = 256


def split_two(value):
    high = value.astype(bf16)
    low = (value - high.astype(f32)).astype(bf16)
    return high, low


def load_rows(ref, filt, blocks, group, filts):
    pieces = [ref[b, pl.ds(filt, group, stride=filts), :] for b in range(blocks)]
    even = jnp.concatenate(pieces[0::2], axis=0)
    odd = jnp.concatenate(pieces[1::2], axis=0)
    return jnp.concatenate([even, odd], axis=1)


def left_fill_roll(value, shift):
    lanes = lax.broadcasted_iota(jnp.int32, value.shape, 1)
    return jnp.where(lanes >= shift, pltpu.roll(value, shift, 1), 0.0)


def signal_kernel(blocks, group, filts, cot_ref, fil_ref, out_ref, high_ref, low_ref):
    local = cot_ref.shape[2]
    pairs = blocks // 2
    length = blocks * local

    def one_filter(filt, carry):
        rows = load_rows(cot_ref, filt, blocks, group, filts)
        lags = jnp.concatenate([fil_ref[b, pl.ds(filt, 1), :] for b in range(blocks)], axis=1)
        first = pltpu.roll(jnp.broadcast_to(lags, (8, length)), 0, 1, stride=1, stride_axis=0)
        lane = lax.broadcasted_iota(jnp.int32, (8, length), 1)
        row = lax.broadcasted_iota(jnp.int32, (8, length), 0)
        first = jnp.where(lane >= row, first, 0.0)
        for step in range(local // 16):
            two = jnp.concatenate(
                [left_fill_roll(first, 16 * step), left_fill_roll(first, 16 * step + 8)], axis=0
            )
            high, low = split_two(two)
            high_ref[pl.ds(16 * step, 16), :] = high
            low_ref[pl.ds(16 * step, 16), :] = low
            pad = jnp.zeros((16, local), bf16)
            high_ref[pl.ds(local + 16 * step, 16), :] = jnp.concatenate([pad, high[:, : length - local]], axis=1)
            low_ref[pl.ds(local + 16 * step, 16), :] = jnp.concatenate([pad, low[:, : length - local]], axis=1)
        total = None
        nt = (((1,), (1,)), ((), ()))
        for gap in range(pairs):
            high, low = split_two(rows[gap * group :, :])
            t_high = high_ref[:, pl.ds(gap * PAIR, PAIR)]
            t_low = low_ref[:, pl.ds(gap * PAIR, PAIR)]
            part = (
                lax.dot_general(high, t_high, nt, preferred_element_type=f32)
                + lax.dot_general(low, t_high, nt, preferred_element_type=f32)
                + lax.dot_general(high, t_low, nt, preferred_element_type=f32)
            )
            if total is None:
                total = part
            else:
                part = jnp.concatenate([part, jnp.zeros((gap * group, PAIR), f32)], axis=0)
                total = total + part
        for b in range(blocks):
            piece = total[(b // 2) * group : (b // 2 + 1) * group, (b % 2) * local : (b % 2 + 1) * local]
            out_ref[b, pl.ds(filt, group, stride=filts), :] = piece
        return carry

    lax.fori_loop(0, filts, one_filter, 0)


def filter_kernel(blocks, group, filts, cot_ref, sig_ref, out_ref, prod_ref):
    local = cot_ref.shape[2]
    pairs = blocks // 2

    def one_filter(filt, carry):
        cot = load_rows(cot_ref, filt, blocks, group, filts)
        sig = load_rows(sig_ref, filt, blocks, group, filts)
        sig_high = sig.astype(bf16).astype(f32)
        stacked = jnp.concatenate([sig_high, sig_high, sig - sig_high], axis=0)
        turned = stacked.T.astype(bf16)
        cot_high = cot.astype(bf16).astype(f32)
        cot_low = cot - cot_high
        for gap in range(pairs):
            pieces = []
            for part in (cot_high, cot_low, cot_high):
                pieces.append(part[gap * group :, :])
                if gap:
                    pieces.append(jnp.zeros((gap * group, PAIR), f32))
            weights = jnp.concatenate(pieces, axis=0).astype(bf16)
            prod_ref[gap] = jnp.dot(turned, weights, preferred_element_type=f32)
        lane = lax.broadcasted_iota(jnp.int32, (8, PAIR), 1)
        sub = lax.broadcasted_iota(jnp.int32, (8, PAIR), 0)
        for gap in range(pairs):
            total = jnp.zeros((8, PAIR), f32)
            for step in reversed(range(PAIR // 8)):
                here = prod_ref[gap, pl.ds(8 * step, 8), :]
                if gap + 1 < pairs:
                    after = prod_ref[gap + 1, pl.ds(8 * step, 8), :]
                else:
                    after = jnp.zeros((8, PAIR), f32)
                kept = jnp.where(lane >= sub + 8 * step, here, after)
                total = pltpu.roll(total, PAIR - 8, 1) + kept
            for bit in (1, 2, 4):
                total = jnp.where((sub & bit) != 0, pltpu.roll(total, PAIR - bit, 1), total)
            total = jnp.sum(total, axis=0, keepdims=True)
            out_ref[2 * gap, pl.ds(filt, 1), :] = total[:, :local]
            out_ref[2 * gap + 1, pl.ds(filt, 1), :] = total[:, local:]
        return carry

    lax.fori_loop(0, filts, one_filter, 0)


def call_signal(cot, fil, group):
    blocks, _, local = cot.shape
    filts = fil.shape[1]
    flops = 2 * 3 * filts * group * (blocks * local) ** 2 // 2
    return pl.pallas_call(
        functools.partial(signal_kernel, blocks, group, filts),
        out_shape=jax.ShapeDtypeStruct(cot.shape, f32),
        in_specs=[pl.BlockSpec(memory_space=pltpu.VMEM)] * 2,
        out_specs=pl.BlockSpec(memory_space=pltpu.VMEM),
        scratch_shapes=[pltpu.VMEM((PAIR, blocks * local), bf16)] * 2,
        compiler_params=pltpu.CompilerParams(vmem_limit_bytes=40 << 20),
        cost_estimate=pl.CostEstimate(flops=flops, bytes_accessed=8 * cot.size, transcendentals=0),
        name="grad_signal",
    )(cot, fil)


def call_filter(cot, sig, group):
    blocks, rows, local = cot.shape
    filts = rows // group
    flops = 2 * 3 * rows * (blocks * local) ** 2
    return pl.pallas_call(
        functools.partial(filter_kernel, blocks, group, filts),
        out_shape=jax.ShapeDtypeStruct((blocks, filts, local), f32),
        in_specs=[pl.BlockSpec(memory_space=pltpu.VMEM)] * 2,
        out_specs=pl.BlockSpec(memory_space=pltpu.VMEM),
        scratch_shapes=[pltpu.VMEM((blocks // 2, PAIR, PAIR), f32)],
        compiler_params=pltpu.CompilerParams(vmem_limit_bytes=40 << 20),
        cost_estimate=pl.CostEstimate(flops=flops, bytes_accessed=8 * cot.size, transcendentals=0),
        name="grad_filters",
    )(cot, sig)


def exchange(value):
    return lax.all_to_all(value, "ctx", split_axis=0, concat_axis=0, tiled=True)


def body(signal, cotangent, filters):
    ranks = lax.axis_size("ctx")
    channels, local = signal.shape
    count = filters.shape[0]
    group = channels // count
    filts = count // ranks

    def by_owner(value):
        return value.reshape(group, ranks, filts, local).transpose(1, 0, 2, 3).reshape(ranks, group * filts, local)

    first = exchange(jnp.concatenate([by_owner(cotangent), filters.reshape(ranks, filts, local)], axis=1))
    sig = exchange(by_owner(signal))
    cot, fil = first[:, : group * filts], first[:, group * filts :]
    dsig = exchange(call_signal(cot, fil, group))
    dfil = call_filter(cot, sig, group)
    if lax.axis_size("tp") == 2:
        dfil = dfil + lax.ppermute(dfil, "tp", [(0, 1), (1, 0)])
    else:
        dfil = lax.psum(dfil, "tp")
    dfil = exchange(dfil)
    grad_signal = dsig.reshape(ranks, group, filts, local).transpose(1, 0, 2, 3).reshape(channels, local)
    return grad_signal, dfil.reshape(count, local)


def solution(mesh):
    return jax.shard_map(
        body,
        mesh=mesh,
        in_specs=(P("tp", "ctx"), P("tp", "ctx"), P(None, "ctx")),
        out_specs=(P("tp", "ctx"), P(None, "ctx")),
        check_vma=False,
    )
```

```python
import functools

import jax
import jax.numpy as jnp
from jax import lax
from jax.experimental import pallas as pl
from jax.experimental.pallas import tpu as pltpu
from jax.sharding import PartitionSpec as P

f32, bf16 = jnp.float32, jnp.bfloat16
PAIR = 256


def split_two(value):
    high = value.astype(bf16)
    low = (value - high.astype(f32)).astype(bf16)
    return high, low


def rotate_left(value, shift):
    half = value.shape[1] // 2
    if shift == half:
        return jnp.concatenate([value[:, half:], value[:, :half]], axis=1)
    return pltpu.roll(value, value.shape[1] - shift, 1)


def load_blocks(ref, start, blocks, sources, group):
    pieces = []
    for b in range(blocks):
        for s in range(sources):
            pieces.append(ref[b * sources + s, pl.ds(start, group), :])
    even = jnp.concatenate([p for at, p in enumerate(pieces) if at // sources % 2 == 0], axis=0)
    odd = jnp.concatenate([p for at, p in enumerate(pieces) if at // sources % 2 == 1], axis=0)
    return jnp.concatenate([even, odd], axis=1)


def gradients_kernel(plan, first_filt, last_filt, *refs):
    blocks, sources, group, filts, early = plan
    if first_filt == 0:
        fil_ref, data_ref, out_ref, strip_high, strip_low, cot_high, cot_low, prod_ref = refs
        fil_at = 2 * early * group
    else:
        fil_ref, data_ref, done_ref, out_ref, strip_high, strip_low, cot_high, cot_low, prod_ref = refs
        fil_at = 2 * early * group
        out_ref[...] = done_ref[...]
    local = data_ref.shape[2]
    count = last_filt - first_filt
    pairs = blocks // 2
    step_rows = sources * group
    rows_all = pairs * step_rows
    length = blocks * local
    held = cot_high.dtype
    flip = lax.broadcasted_iota(jnp.int32, (local, local), 0) + lax.broadcasted_iota(jnp.int32, (local, local), 1)
    flip = jnp.where(flip == local - 1, 1.0, 0.0).astype(bf16)
    for ref in (cot_high, cot_low):
        ref[pl.ds(rows_all, rows_all), :] = jnp.zeros((rows_all, PAIR), held)
    prod_ref[pairs] = jnp.zeros((PAIR, PAIR), f32)
    lane = lax.broadcasted_iota(jnp.int32, (8, PAIR), 1)
    sub = lax.broadcasted_iota(jnp.int32, (8, PAIR), 0)
    ahead = lane - sub

    def one_filter(turn, carry):
        filt = first_filt + turn
        rows = load_blocks(data_ref, turn * group, blocks, sources, group)
        high, low = split_two(rows)
        cot_high[pl.ds(0, rows_all), :] = high.astype(held)
        cot_low[pl.ds(0, rows_all), :] = low.astype(held)

        lags = [fil_ref[b * sources, pl.ds(fil_at + filt, 1), :] for b in reversed(range(blocks))]
        high, low = split_two(jnp.concatenate(lags, axis=0))
        back = jnp.dot(high, flip, preferred_element_type=f32) + jnp.dot(low, flip, preferred_element_type=f32)
        back = [jnp.broadcast_to(back[b : b + 1, :], (8, local)) for b in range(blocks)]
        back = jnp.concatenate(back + [jnp.zeros((8, PAIR), f32)], axis=1)
        skewed = pltpu.roll(back, 1, 1, stride=1, stride_axis=0)
        for step in range(local // 16):
            two = jnp.concatenate([pltpu.roll(skewed, 16 * step, 1), pltpu.roll(skewed, 16 * step + 8, 1)], axis=0)
            high, low = split_two(two)
            strip_high[pl.ds(16 * step, 16), :] = high
            strip_low[pl.ds(16 * step, 16), :] = low

        sig = load_blocks(data_ref, (count + turn) * group, blocks, sources, group).T
        sig_high, sig_low = split_two(sig)
        turned = jnp.concatenate([sig_high, sig_high, sig_low], axis=1)
        for gap in range(pairs):
            high = cot_high[pl.ds(gap * step_rows, rows_all), :].astype(bf16)
            low = cot_low[pl.ds(gap * step_rows, rows_all), :].astype(bf16)
            weights = jnp.concatenate([high, low, high], axis=0)
            prod_ref[gap] = jnp.dot(turned, weights, preferred_element_type=f32)

        total = None
        for gap in range(pairs):
            kept = rows_all - gap * step_rows
            high = cot_high[pl.ds(gap * step_rows, kept), :].astype(bf16)
            low = cot_low[pl.ds(gap * step_rows, kept), :].astype(bf16)
            at = length - gap * PAIR
            t_high = jnp.concatenate([strip_high[:, pl.ds(at, PAIR)], strip_high[:, pl.ds(at - local, PAIR)]], axis=0)
            t_low = jnp.concatenate([strip_low[:, pl.ds(at, PAIR)], strip_low[:, pl.ds(at - local, PAIR)]], axis=0)
            part = (
                jnp.dot(high, t_high, preferred_element_type=f32)
                + jnp.dot(low, t_high, preferred_element_type=f32)
                + jnp.dot(high, t_low, preferred_element_type=f32)
            )
            if total is None:
                total = part
            else:
                part = jnp.concatenate([part, jnp.zeros((gap * step_rows, PAIR), f32)], axis=0)
                total = total + part
        for b in range(blocks):
            for s in range(sources):
                at = b // 2 * step_rows + s * group
                piece = total[at : at + group, b % 2 * local : (b % 2 + 1) * local]
                out_ref[b * sources + s, pl.ds(filt * group, group), :] = piece

        def folded(gap, step, steps):
            if steps == 1:
                here = prod_ref[gap, pl.ds(8 * step, 8), :]
                after = prod_ref[gap + 1, pl.ds(8 * step, 8), :]
                return jnp.where(ahead >= 8 * step, here, after)
            half = steps // 2
            return folded(gap, step, half) + rotate_left(folded(gap, step + half, half), 8 * half)

        for gap in range(pairs):
            lagged = folded(gap, 0, PAIR // 8)
            for bit in (1, 2, 4):
                lagged = jnp.where((sub & bit) != 0, rotate_left(lagged, bit), lagged)
            lagged = jnp.sum(lagged, axis=0, keepdims=True)
            for s in range(sources):
                out_ref[2 * gap * sources + s, pl.ds(filts * group + filt, 1), :] = lagged[:, :local]
                out_ref[(2 * gap + 1) * sources + s, pl.ds(filts * group + filt, 1), :] = lagged[:, local:]
        return carry

    lax.fori_loop(0, count, one_filter, 0)


def vmem_call(kernel, outs, args, name, flops, scratch=()):
    return pl.pallas_call(
        kernel,
        out_shape=outs,
        in_specs=[pl.BlockSpec(memory_space=pltpu.VMEM)] * len(args),
        out_specs=jax.tree.map(lambda _: pl.BlockSpec(memory_space=pltpu.VMEM), outs),
        scratch_shapes=list(scratch),
        compiler_params=pltpu.CompilerParams(vmem_limit_bytes=44 << 20),
        cost_estimate=pl.CostEstimate(
            flops=int(flops), bytes_accessed=sum(4 * a.size for a in args), transcendentals=0
        ),
        name=name,
    )(*args)


def call_gradients(plan, first_filt, last_filt, *args):
    blocks, sources, group, filts, early = plan
    local = args[0].shape[2]
    rows = blocks * sources * group
    held = bf16 if sources * group % 16 == 0 else f32
    scratch = (
        [pltpu.VMEM((local, blocks * local + PAIR), bf16)] * 2
        + [pltpu.VMEM((rows, PAIR), held)] * 2
        + [pltpu.VMEM((blocks // 2 + 1, PAIR, PAIR), f32)]
    )
    outs = jax.ShapeDtypeStruct((blocks * sources, filts * group + filts, local), f32)
    kernel = functools.partial(gradients_kernel, plan, first_filt, last_filt)
    flops = (last_filt - first_filt) * 3e9
    return vmem_call(kernel, outs, args, "gradients", flops, scratch)


def pack_kernel(plan, owners, cot_ref, sig_ref, fil_ref, early_ref, late_ref):
    _, _, group, filts, early = plan
    count = owners * filts

    def one_owner(owner, carry):
        for filt in range(filts):
            ref, at, many = (early_ref, filt, early) if filt < early else (late_ref, filt - early, filts - early)
            for part, source in enumerate((cot_ref, sig_ref)):
                rows = source[pl.ds(owner * filts + filt, group, stride=count), :]
                ref[owner, pl.ds((part * many + at) * group, group), :] = rows
        early_ref[owner, pl.ds(2 * early * group, filts), :] = fil_ref[pl.ds(owner * filts, filts), :]
        return carry

    lax.fori_loop(0, owners, one_owner, 0)


def unpack_kernel(plan, owners, in_ref, sig_ref, fil_ref):
    _, _, group, filts, _ = plan
    count = owners * filts

    def one_owner(owner, carry):
        for filt in range(filts):
            sig_ref[pl.ds(owner * filts + filt, group, stride=count), :] = in_ref[owner, pl.ds(filt * group, group), :]
        fil_ref[pl.ds(owner * filts, filts), :] = in_ref[owner, pl.ds(filts * group, filts), :]
        return carry

    lax.fori_loop(0, owners, one_owner, 0)


def body(signal, cotangent, filters):
    ranks, halves = lax.axis_size("ctx"), lax.axis_size("tp")
    channels, local = signal.shape
    count = filters.shape[0]
    both = count % (8 * ranks * halves) == 0
    axes, sources = (("ctx", "tp"), halves) if both else ("ctx", 1)
    owners = ranks * sources
    group, filts = channels // count, count // owners
    early = filts - filts // 4
    plan = (ranks, sources, group, filts, early)

    def exchange(value):
        return lax.all_to_all(value, axes, split_axis=0, concat_axis=0, tiled=True)

    sizes = (2 * early * group + filts, 2 * (filts - early) * group)
    sends = vmem_call(
        functools.partial(pack_kernel, plan, owners),
        [jax.ShapeDtypeStruct((owners, rows, local), f32) for rows in sizes],
        (cotangent, signal, filters),
        "pack_rows",
        1e6,
    )
    first = exchange(sends[0])
    first, late = lax.optimization_barrier((first, sends[1]))
    second = exchange(late)
    grads = call_gradients(plan, 0, early, first, first)
    grads = call_gradients(plan, early, filts, first, second, grads)
    grad_signal, grad_filters = vmem_call(
        functools.partial(unpack_kernel, plan, owners),
        [jax.ShapeDtypeStruct((channels, local), f32), jax.ShapeDtypeStruct((count, local), f32)],
        (exchange(grads),),
        "unpack_rows",
        1e6,
    )
    if not both:
        grad_filters = lax.psum(grad_filters, "tp")
    return grad_signal, grad_filters


def solution(mesh):
    return jax.shard_map(
        body,
        mesh=mesh,
        in_specs=(P("tp", "ctx"), P("tp", "ctx"), P(None, "ctx")),
        out_specs=(P("tp", "ctx"), P(None, "ctx")),
        check_vma=False,
    )
```

```python
import functools
import math

import jax
import jax.numpy as jnp
from jax import lax
from jax.experimental import pallas as pl
from jax.experimental.pallas import tpu as pltpu
from jax.sharding import PartitionSpec as P

f32, bf16 = jnp.float32, jnp.bfloat16
PAIR = 256


def split_two(value):
    high = value.astype(bf16)
    low = (value - high.astype(f32)).astype(bf16)
    return high, low


def rotate_left(value, shift):
    half = value.shape[1] // 2
    if shift == half:
        return jnp.concatenate([value[:, half:], value[:, :half]], axis=1)
    return pltpu.roll(value, value.shape[1] - shift, 1)


def load_blocks(ref, start, blocks, sources, group):
    pieces = []
    for b in range(blocks):
        for s in range(sources):
            pieces.append(ref[b * sources + s, pl.ds(start, group), :])
    even = jnp.concatenate([p for at, p in enumerate(pieces) if at // sources % 2 == 0], axis=0)
    odd = jnp.concatenate([p for at, p in enumerate(pieces) if at // sources % 2 == 1], axis=0)
    return jnp.concatenate([even, odd], axis=1)


def gradients_kernel(plan, first_filt, last_filt, *refs):
    blocks, sources, group, filts, early = plan
    if first_filt == 0:
        fil_ref, data_ref, out_ref, strip_high, strip_low, cot_high, cot_low, prod_ref = refs
        fil_at = 2 * early * group
    else:
        fil_ref, data_ref, done_ref, out_ref, strip_high, strip_low, cot_high, cot_low, prod_ref = refs
        fil_at = 2 * early * group
        out_ref[...] = done_ref[...]
    local = data_ref.shape[2]
    count = last_filt - first_filt
    pairs = blocks // 2
    step_rows = sources * group
    rows_all = pairs * step_rows
    length = blocks * local
    held = cot_high.dtype
    flip = lax.broadcasted_iota(jnp.int32, (local, local), 0) + lax.broadcasted_iota(jnp.int32, (local, local), 1)
    flip = jnp.where(flip == local - 1, 1.0, 0.0).astype(bf16)
    for ref in (cot_high, cot_low):
        ref[pl.ds(rows_all, rows_all), :] = jnp.zeros((rows_all, PAIR), held)
    prod_ref[pairs] = jnp.zeros((PAIR, PAIR), f32)
    lane = lax.broadcasted_iota(jnp.int32, (8, PAIR), 1)
    sub = lax.broadcasted_iota(jnp.int32, (8, PAIR), 0)
    ahead = lane - sub

    def one_filter(turn, carry):
        filt = first_filt + turn
        rows = load_blocks(data_ref, turn * group, blocks, sources, group)
        high, low = split_two(rows)
        cot_high[pl.ds(0, rows_all), :] = high.astype(held)
        cot_low[pl.ds(0, rows_all), :] = low.astype(held)

        lags = [fil_ref[b * sources, pl.ds(fil_at + filt, 1), :] for b in reversed(range(blocks))]
        high, low = split_two(jnp.concatenate(lags, axis=0))
        back = jnp.dot(high, flip, preferred_element_type=f32) + jnp.dot(low, flip, preferred_element_type=f32)
        back = [jnp.broadcast_to(back[b : b + 1, :], (8, local)) for b in range(blocks)]
        back = jnp.concatenate(back + [jnp.zeros((8, PAIR), f32)], axis=1)
        skewed = pltpu.roll(back, 1, 1, stride=1, stride_axis=0)
        for step in range(local // 16):
            two = jnp.concatenate([pltpu.roll(skewed, 16 * step, 1), pltpu.roll(skewed, 16 * step + 8, 1)], axis=0)
            high, low = split_two(two)
            strip_high[pl.ds(16 * step, 16), :] = high
            strip_low[pl.ds(16 * step, 16), :] = low

        sig = load_blocks(data_ref, (count + turn) * group, blocks, sources, group).T
        sig_high, sig_low = split_two(sig)
        turned = jnp.concatenate([sig_high, sig_high, sig_low], axis=1)
        for gap in range(pairs):
            high = cot_high[pl.ds(gap * step_rows, rows_all), :].astype(bf16)
            low = cot_low[pl.ds(gap * step_rows, rows_all), :].astype(bf16)
            weights = jnp.concatenate([high, low, high], axis=0)
            prod_ref[gap] = jnp.dot(turned, weights, preferred_element_type=f32)

        total = None
        for gap in range(pairs):
            kept = rows_all - gap * step_rows
            high = cot_high[pl.ds(gap * step_rows, kept), :].astype(bf16)
            low = cot_low[pl.ds(gap * step_rows, kept), :].astype(bf16)
            at = length - gap * PAIR
            t_high = jnp.concatenate([strip_high[:, pl.ds(at, PAIR)], strip_high[:, pl.ds(at - local, PAIR)]], axis=0)
            t_low = jnp.concatenate([strip_low[:, pl.ds(at, PAIR)], strip_low[:, pl.ds(at - local, PAIR)]], axis=0)
            part = (
                jnp.dot(high, t_high, preferred_element_type=f32)
                + jnp.dot(low, t_high, preferred_element_type=f32)
                + jnp.dot(high, t_low, preferred_element_type=f32)
            )
            if total is None:
                total = part
            else:
                part = jnp.concatenate([part, jnp.zeros((gap * step_rows, PAIR), f32)], axis=0)
                total = total + part
        for b in range(blocks):
            for s in range(sources):
                at = b // 2 * step_rows + s * group
                piece = total[at : at + group, b % 2 * local : (b % 2 + 1) * local]
                out_ref[b * sources + s, pl.ds(filt * group, group), :] = piece

        def folded(gap, step, steps):
            if steps == 1:
                here = prod_ref[gap, pl.ds(8 * step, 8), :]
                after = prod_ref[gap + 1, pl.ds(8 * step, 8), :]
                return jnp.where(ahead >= 8 * step, here, after)
            half = steps // 2
            return folded(gap, step, half) + rotate_left(folded(gap, step + half, half), 8 * half)

        for gap in range(pairs):
            lagged = folded(gap, 0, PAIR // 8)
            for bit in (1, 2, 4):
                lagged = jnp.where((sub & bit) != 0, rotate_left(lagged, bit), lagged)
            lagged = jnp.sum(lagged, axis=0, keepdims=True)
            for s in range(sources):
                out_ref[2 * gap * sources + s, pl.ds(filts * group + filt, 1), :] = lagged[:, :local]
                out_ref[(2 * gap + 1) * sources + s, pl.ds(filts * group + filt, 1), :] = lagged[:, local:]
        return carry

    lax.fori_loop(0, count, one_filter, 0)


def vmem_call(kernel, outs, args, name, flops, scratch=()):
    return pl.pallas_call(
        kernel,
        out_shape=outs,
        in_specs=[pl.BlockSpec(memory_space=pltpu.VMEM)] * len(args),
        out_specs=jax.tree.map(lambda _: pl.BlockSpec(memory_space=pltpu.VMEM), outs),
        scratch_shapes=list(scratch),
        compiler_params=pltpu.CompilerParams(vmem_limit_bytes=44 << 20),
        cost_estimate=pl.CostEstimate(
            flops=int(flops), bytes_accessed=sum(4 * a.size for a in args), transcendentals=0
        ),
        name=name,
    )(*args)


def call_gradients(plan, first_filt, last_filt, *args):
    blocks, sources, group, filts, early = plan
    local = args[0].shape[2]
    rows = blocks * sources * group
    held = bf16 if sources * group % 16 == 0 else f32
    scratch = (
        [pltpu.VMEM((local, blocks * local + PAIR), bf16)] * 2
        + [pltpu.VMEM((rows, PAIR), held)] * 2
        + [pltpu.VMEM((blocks // 2 + 1, PAIR, PAIR), f32)]
    )
    outs = jax.ShapeDtypeStruct((blocks * sources, filts * group + filts, local), f32)
    kernel = functools.partial(gradients_kernel, plan, first_filt, last_filt)
    flops = (last_filt - first_filt) * 3e9
    return vmem_call(kernel, outs, args, "gradients", flops, scratch)


def pack_kernel(plan, owners, cot_ref, sig_ref, fil_ref, early_ref, late_ref):
    _, _, group, filts, early = plan
    count = owners * filts

    def one_owner(owner, carry):
        for filt in range(filts):
            ref, at, many = (early_ref, filt, early) if filt < early else (late_ref, filt - early, filts - early)
            for part, source in enumerate((cot_ref, sig_ref)):
                rows = source[pl.ds(owner * filts + filt, group, stride=count), :]
                ref[owner, pl.ds((part * many + at) * group, group), :] = rows
        early_ref[owner, pl.ds(2 * early * group, filts), :] = fil_ref[pl.ds(owner * filts, filts), :]
        return carry

    lax.fori_loop(0, owners, one_owner, 0)


def unpack_kernel(plan, owners, in_ref, sig_ref, fil_ref):
    _, _, group, filts, _ = plan
    count = owners * filts

    def one_owner(owner, carry):
        for filt in range(filts):
            sig_ref[pl.ds(owner * filts + filt, group, stride=count), :] = in_ref[owner, pl.ds(filt * group, group), :]
        fil_ref[pl.ds(owner * filts, filts), :] = in_ref[owner, pl.ds(filts * group, filts), :]
        return carry

    lax.fori_loop(0, owners, one_owner, 0)


def turn_blocks(value):
    rows = [value[at] for at in range(8)]
    sub = lax.broadcasted_iota(jnp.int32, rows[0].shape, 0)
    for bit in (1, 2, 4):
        clear = (sub & bit) == 0
        turned = list(rows)
        for at in range(8):
            if at & bit == 0:
                turned[at] = jnp.where(clear, rows[at], pltpu.roll(rows[at + bit], bit, 0))
                turned[at + bit] = jnp.where(clear, pltpu.roll(rows[at], 8 - bit, 0), rows[at + bit])
        rows = turned
    return rows


def pack_copied_kernel(plan, owners, chunks, cot_hbm, sig_hbm, fil_hbm, early_ref, late_ref, cot_ref, sig_ref, sems, fil_sem):
    _, _, group, filts, early = plan
    many = owners // chunks
    span = many * filts
    copies = []
    for chunk in range(chunks):
        for part, (source, target) in enumerate(((cot_hbm, cot_ref), (sig_hbm, sig_ref))):
            rows = pl.ds(chunk * span, span)
            copies.append(pltpu.make_async_copy(source.at[:, rows, :], target.at[:, rows, :], sems.at[part, chunk]))
            copies[-1].start()
    fil_copy = pltpu.make_async_copy(fil_hbm, early_ref.at[:, pl.ds(2 * early * group, filts), :], fil_sem)
    fil_copy.start()
    for chunk in range(chunks):
        for part, source in enumerate((cot_ref, sig_ref)):
            copies[2 * chunk + part].wait()
            for owner in range(chunk * many, (chunk + 1) * many):
                rows = turn_blocks(source[:, pl.ds(owner * filts, filts), :])
                for filt in range(filts):
                    if filt < early:
                        early_ref[owner, pl.ds((part * early + filt) * group, group), :] = rows[filt]
                    else:
                        at = part * (filts - early) + filt - early
                        late_ref[owner, pl.ds(at * group, group), :] = rows[filt]
    fil_copy.wait()


def unpack_copied_kernel(plan, owners, chunks, in_ref, sig_hbm, fil_hbm, sig_ref, sems, fil_sem):
    _, _, group, filts, _ = plan
    many = owners // chunks
    span = many * filts
    fil_copy = pltpu.make_async_copy(in_ref.at[:, pl.ds(filts * group, filts), :], fil_hbm, fil_sem)
    fil_copy.start()
    copies = []
    for chunk in range(chunks):
        for owner in range(chunk * many, (chunk + 1) * many):
            block = jnp.stack([in_ref[owner, pl.ds(filt * group, group), :] for filt in range(filts)], axis=0)
            for at, row in enumerate(turn_blocks(block)):
                sig_ref[at, pl.ds(owner * filts, filts), :] = row
        rows = pl.ds(chunk * span, span)
        copies.append(pltpu.make_async_copy(sig_ref.at[:, rows, :], sig_hbm.at[:, rows, :], sems.at[chunk]))
        copies[-1].start()
    for copy in copies:
        copy.wait()
    fil_copy.wait()


def pack_rows(plan, owners, sizes, cot, sig, fil):
    _, _, group, filts, _ = plan
    channels, local = cot.shape
    outs = [jax.ShapeDtypeStruct((owners, rows, local), f32) for rows in sizes]
    if (group, filts) != (8, 8):
        return vmem_call(functools.partial(pack_kernel, plan, owners), outs, (cot, sig, fil), "pack_rows", 1e6)
    chunks = math.gcd(owners, 4)
    grouped = (group, channels // group, local)
    return pl.pallas_call(
        functools.partial(pack_copied_kernel, plan, owners, chunks),
        out_shape=outs,
        in_specs=[pl.BlockSpec(memory_space=pl.ANY)] * 3,
        out_specs=[pl.BlockSpec(memory_space=pltpu.VMEM)] * 2,
        scratch_shapes=[pltpu.VMEM(grouped, f32)] * 2
        + [pltpu.SemaphoreType.DMA((2, chunks)), pltpu.SemaphoreType.DMA],
        compiler_params=pltpu.CompilerParams(vmem_limit_bytes=61 << 20),
        cost_estimate=pl.CostEstimate(flops=0, bytes_accessed=16 * cot.size, transcendentals=0),
        name="pack_rows",
    )(cot.reshape(grouped), sig.reshape(grouped), fil.reshape(owners, filts, local))


def unpack_rows(plan, owners, value):
    _, _, group, filts, _ = plan
    count, local = owners * filts, value.shape[2]
    channels = group * count
    if (group, filts) != (8, 8):
        outs = [jax.ShapeDtypeStruct((channels, local), f32), jax.ShapeDtypeStruct((count, local), f32)]
        return vmem_call(functools.partial(unpack_kernel, plan, owners), outs, (value,), "unpack_rows", 1e6)
    chunks = math.gcd(owners, 4)
    grouped = (group, count, local)
    dsig, dfil = pl.pallas_call(
        functools.partial(unpack_copied_kernel, plan, owners, chunks),
        out_shape=[jax.ShapeDtypeStruct(grouped, f32), jax.ShapeDtypeStruct((owners, filts, local), f32)],
        in_specs=[pl.BlockSpec(memory_space=pltpu.VMEM)],
        out_specs=[pl.BlockSpec(memory_space=pl.ANY)] * 2,
        scratch_shapes=[pltpu.VMEM(grouped, f32), pltpu.SemaphoreType.DMA((chunks,)), pltpu.SemaphoreType.DMA],
        compiler_params=pltpu.CompilerParams(vmem_limit_bytes=44 << 20),
        cost_estimate=pl.CostEstimate(flops=0, bytes_accessed=8 * value.size, transcendentals=0),
        name="unpack_rows",
    )(value)
    return dsig.reshape(channels, local), dfil.reshape(count, local)


def body(signal, cotangent, filters):
    ranks, halves = lax.axis_size("ctx"), lax.axis_size("tp")
    channels, local = signal.shape
    count = filters.shape[0]
    both = count % (8 * ranks * halves) == 0
    axes, sources = (("ctx", "tp"), halves) if both else ("ctx", 1)
    owners = ranks * sources
    group, filts = channels // count, count // owners
    early = filts - filts // 4
    plan = (ranks, sources, group, filts, early)

    def exchange(value):
        return lax.all_to_all(value, axes, split_axis=0, concat_axis=0, tiled=True)

    sizes = (2 * early * group + filts, 2 * (filts - early) * group)
    sends = pack_rows(plan, owners, sizes, cotangent, signal, filters)
    first = exchange(sends[0])
    first, late = lax.optimization_barrier((first, sends[1]))
    second = exchange(late)
    grads = call_gradients(plan, 0, early, first, first)
    grads = call_gradients(plan, early, filts, first, second, grads)
    grad_signal, grad_filters = unpack_rows(plan, owners, exchange(grads))
    if not both:
        grad_filters = lax.psum(grad_filters, "tp")
    return grad_signal, grad_filters


def solution(mesh):
    return jax.shard_map(
        body,
        mesh=mesh,
        in_specs=(P("tp", "ctx"), P("tp", "ctx"), P(None, "ctx")),
        out_specs=(P("tp", "ctx"), P(None, "ctx")),
        check_vma=False,
    )
```

```python
import functools
import math

import jax
import jax.numpy as jnp
from jax import lax
from jax.experimental import pallas as pl
from jax.experimental.pallas import tpu as pltpu
from jax.sharding import PartitionSpec as P

f32, bf16 = jnp.float32, jnp.bfloat16
PAIR = 256


def split_two(value):
    high = value.astype(bf16)
    low = (value - high.astype(f32)).astype(bf16)
    return high, low


def rotate_left(value, shift):
    half = value.shape[1] // 2
    if shift == half:
        return jnp.concatenate([value[:, half:], value[:, :half]], axis=1)
    return pltpu.roll(value, value.shape[1] - shift, 1)


def load_blocks(ref, start, blocks, sources, group):
    pieces = []
    for b in range(blocks):
        for s in range(sources):
            pieces.append(ref[b * sources + s, pl.ds(start, group), :])
    even = jnp.concatenate([p for at, p in enumerate(pieces) if at // sources % 2 == 0], axis=0)
    odd = jnp.concatenate([p for at, p in enumerate(pieces) if at // sources % 2 == 1], axis=0)
    return jnp.concatenate([even, odd], axis=1)


def gradients_kernel(plan, first_filt, last_filt, *refs):
    blocks, sources, group, filts, early = plan
    if first_filt == 0:
        fil_ref, data_ref, out_ref, strip_high, strip_low, cot_high, cot_low, weight_ref, prod_ref = refs
        fil_at = 2 * early * group
    else:
        fil_ref, data_ref, done_ref, out_ref, strip_high, strip_low, cot_high, cot_low, weight_ref, prod_ref = refs
        fil_at = 2 * early * group
        out_ref[...] = done_ref[...]
    local = data_ref.shape[2]
    count = last_filt - first_filt
    pairs = blocks // 2
    step_rows = sources * group
    rows_all = pairs * step_rows
    length = blocks * local
    held = cot_high.dtype
    flip = lax.broadcasted_iota(jnp.int32, (local, local), 0) + lax.broadcasted_iota(jnp.int32, (local, local), 1)
    flip = jnp.where(flip == local - 1, 1.0, 0.0).astype(bf16)
    weight_ref[pl.ds(3 * rows_all, 256), :] = jnp.zeros((256, PAIR), held)
    prod_ref[pairs] = jnp.zeros((PAIR, PAIR), f32)
    lane = lax.broadcasted_iota(jnp.int32, (8, PAIR), 1)
    sub = lax.broadcasted_iota(jnp.int32, (8 * pairs, PAIR), 0)
    ahead = lane[:, :128] - sub[:8, :128]

    def one_filter(turn, carry):
        filt = first_filt + turn
        rows = load_blocks(data_ref, turn * group, blocks, sources, group)
        high, low = split_two(rows)
        cot_high[pl.ds(0, rows_all), :] = high.astype(held)
        cot_low[pl.ds(0, rows_all), :] = low.astype(held)
        for at in range(0, rows_all, step_rows):
            for turn_at, part in enumerate((high, low, high)):
                weight_ref[pl.ds(3 * at + turn_at * step_rows, step_rows), :] = part[at : at + step_rows].astype(held)

        lags = [fil_ref[b * sources, pl.ds(fil_at + filt, 1), :] for b in reversed(range(blocks))]
        high, low = split_two(jnp.concatenate(lags, axis=0))
        back = jnp.dot(high, flip, preferred_element_type=f32) + jnp.dot(low, flip, preferred_element_type=f32)
        back = [jnp.broadcast_to(back[b : b + 1, :], (8, local)) for b in range(blocks)]
        back = jnp.concatenate(back + [jnp.zeros((8, PAIR), f32)], axis=1)
        skewed = pltpu.roll(back, 1, 1, stride=1, stride_axis=0)
        two = jnp.concatenate([skewed, pltpu.roll(skewed, 8, 1)], axis=0)
        high, low = split_two(two)
        high, low = high.astype(f32), low.astype(f32)
        for step in range(local // 16):
            strip_high[pl.ds(16 * step, 16), :] = pltpu.roll(high, 16 * step, 1).astype(bf16)
            strip_low[pl.ds(16 * step, 16), :] = pltpu.roll(low, 16 * step, 1).astype(bf16)

        sig = load_blocks(data_ref, (count + turn) * group, blocks, sources, group)
        sig_high = sig.astype(bf16).astype(f32)
        sig_low = sig - sig_high
        stacked = []
        for at in range(0, rows_all, step_rows):
            stacked += [part[at : at + step_rows] for part in (sig_high, sig_high, sig_low)]
        turned = jnp.concatenate(stacked, axis=0).T.astype(bf16)
        for gap in range(pairs):
            deep = min(-(-3 * (rows_all - gap * step_rows) // 256) * 256, 3 * rows_all)
            weights = weight_ref[pl.ds(3 * gap * step_rows, deep), :].astype(bf16)
            prod_ref[gap] = jnp.dot(turned[:, :deep], weights, preferred_element_type=f32)

        total = None
        for gap in range(pairs):
            kept = rows_all - gap * step_rows
            high = cot_high[pl.ds(gap * step_rows, kept), :].astype(bf16)
            low = cot_low[pl.ds(gap * step_rows, kept), :].astype(bf16)
            at = length - gap * PAIR
            t_high = jnp.concatenate([strip_high[:, pl.ds(at, PAIR)], strip_high[:, pl.ds(at - local, PAIR)]], axis=0)
            t_low = jnp.concatenate([strip_low[:, pl.ds(at, PAIR)], strip_low[:, pl.ds(at - local, PAIR)]], axis=0)
            both = jnp.dot(jnp.concatenate([high, low], axis=0), t_high, preferred_element_type=f32)
            part = both[:kept] + both[kept:] + jnp.dot(high, t_low, preferred_element_type=f32)
            if total is None:
                total = part
            else:
                part = jnp.concatenate([part, jnp.zeros((gap * step_rows, PAIR), f32)], axis=0)
                total = total + part
        for b in range(blocks):
            for s in range(sources):
                at = b // 2 * step_rows + s * group
                piece = total[at : at + group, b % 2 * local : (b % 2 + 1) * local]
                out_ref[b * sources + s, pl.ds(filt * group, group), :] = piece

        def leaf(gap, step):
            near, far = pl.ds(8 * step, 8), pl.ds(8 * step + 128, 8)
            left, right = pl.ds(0, 128), pl.ds(128, 128)
            valid = ahead >= 8 * step
            first = jnp.where(valid, prod_ref[gap, near, left], prod_ref[gap + 1, near, left])
            second = jnp.where(valid, prod_ref[gap, far, right], prod_ref[gap + 1, far, right])
            return jnp.concatenate([first + second, prod_ref[gap, near, right] + prod_ref[gap + 1, far, left]], axis=1)

        lagged = []
        for gap in range(pairs):
            summed = leaf(gap, 0)
            for step in range(1, PAIR // 16):
                summed = summed + rotate_left(leaf(gap, step), 8 * step)
            lagged.append(summed)
        lagged = jnp.concatenate(lagged, axis=0)
        for bit in (1, 2, 4):
            lagged = jnp.where((sub & bit) != 0, rotate_left(lagged, bit), lagged)
        lagged = jnp.sum(lagged.reshape(pairs, 8, PAIR), axis=1)
        for gap in range(pairs):
            for s in range(sources):
                row = pl.ds(filts * group + filt, 1)
                out_ref[2 * gap * sources + s, row, :] = lagged[gap : gap + 1, :local]
                out_ref[(2 * gap + 1) * sources + s, row, :] = lagged[gap : gap + 1, local:]
        return carry

    lax.fori_loop(0, count, one_filter, 0)


def vmem_call(kernel, outs, args, name, flops, scratch=()):
    return pl.pallas_call(
        kernel,
        out_shape=outs,
        in_specs=[pl.BlockSpec(memory_space=pltpu.VMEM)] * len(args),
        out_specs=jax.tree.map(lambda _: pl.BlockSpec(memory_space=pltpu.VMEM), outs),
        scratch_shapes=list(scratch),
        compiler_params=pltpu.CompilerParams(vmem_limit_bytes=44 << 20),
        cost_estimate=pl.CostEstimate(
            flops=int(flops), bytes_accessed=sum(4 * a.size for a in args), transcendentals=0
        ),
        name=name,
    )(*args)


def call_gradients(plan, first_filt, last_filt, *args):
    blocks, sources, group, filts, early = plan
    local = args[0].shape[2]
    rows = blocks * sources * group
    held = bf16 if sources * group % 16 == 0 else f32
    scratch = (
        [pltpu.VMEM((local, blocks * local + PAIR), bf16)] * 2
        + [pltpu.VMEM((rows // 2, PAIR), held)] * 2
        + [pltpu.VMEM((3 * rows // 2 + 256, PAIR), held), pltpu.VMEM((blocks // 2 + 1, PAIR, PAIR), f32)]
    )
    outs = jax.ShapeDtypeStruct((blocks * sources, filts * group + filts, local), f32)
    kernel = functools.partial(gradients_kernel, plan, first_filt, last_filt)
    flops = (last_filt - first_filt) * 3e9
    return vmem_call(kernel, outs, args, "gradients", flops, scratch)


def pack_kernel(plan, owners, cot_ref, sig_ref, fil_ref, early_ref, late_ref):
    _, _, group, filts, early = plan
    count = owners * filts

    def one_owner(owner, carry):
        for filt in range(filts):
            ref, at, many = (early_ref, filt, early) if filt < early else (late_ref, filt - early, filts - early)
            for part, source in enumerate((cot_ref, sig_ref)):
                rows = source[pl.ds(owner * filts + filt, group, stride=count), :]
                ref[owner, pl.ds((part * many + at) * group, group), :] = rows
        early_ref[owner, pl.ds(2 * early * group, filts), :] = fil_ref[pl.ds(owner * filts, filts), :]
        return carry

    lax.fori_loop(0, owners, one_owner, 0)


def unpack_kernel(plan, owners, in_ref, sig_ref, fil_ref):
    _, _, group, filts, _ = plan
    count = owners * filts

    def one_owner(owner, carry):
        for filt in range(filts):
            sig_ref[pl.ds(owner * filts + filt, group, stride=count), :] = in_ref[owner, pl.ds(filt * group, group), :]
        fil_ref[pl.ds(owner * filts, filts), :] = in_ref[owner, pl.ds(filts * group, filts), :]
        return carry

    lax.fori_loop(0, owners, one_owner, 0)


def turn_blocks(value):
    rows = [value[at] for at in range(8)]
    sub = lax.broadcasted_iota(jnp.int32, rows[0].shape, 0)
    for bit in (1, 2, 4):
        clear = (sub & bit) == 0
        turned = list(rows)
        for at in range(8):
            if at & bit == 0:
                turned[at] = jnp.where(clear, rows[at], pltpu.roll(rows[at + bit], bit, 0))
                turned[at + bit] = jnp.where(clear, pltpu.roll(rows[at], 8 - bit, 0), rows[at + bit])
        rows = turned
    return rows


def pack_copied_kernel(plan, owners, chunks, cot_hbm, sig_hbm, fil_hbm, early_ref, late_ref, cot_ref, sig_ref, sems, fil_sem):
    _, _, group, filts, early = plan
    many = owners // chunks
    span = many * filts
    copies = []
    for chunk in range(chunks):
        for part, (source, target) in enumerate(((cot_hbm, cot_ref), (sig_hbm, sig_ref))):
            rows = pl.ds(chunk * span, span)
            copies.append(pltpu.make_async_copy(source.at[:, rows, :], target.at[:, rows, :], sems.at[part, chunk]))
            copies[-1].start()
    fil_copy = pltpu.make_async_copy(fil_hbm, early_ref.at[:, pl.ds(2 * early * group, filts), :], fil_sem)
    fil_copy.start()
    for chunk in range(chunks):
        for part, source in enumerate((cot_ref, sig_ref)):
            copies[2 * chunk + part].wait()
            for owner in range(chunk * many, (chunk + 1) * many):
                rows = turn_blocks(source[:, pl.ds(owner * filts, filts), :])
                for filt in range(filts):
                    if filt < early:
                        early_ref[owner, pl.ds((part * early + filt) * group, group), :] = rows[filt]
                    else:
                        at = part * (filts - early) + filt - early
                        late_ref[owner, pl.ds(at * group, group), :] = rows[filt]
    fil_copy.wait()


def unpack_copied_kernel(plan, owners, chunks, in_ref, sig_hbm, fil_hbm, sig_ref, sems, fil_sem):
    _, _, group, filts, _ = plan
    many = owners // chunks
    span = many * filts
    fil_copy = pltpu.make_async_copy(in_ref.at[:, pl.ds(filts * group, filts), :], fil_hbm, fil_sem)
    fil_copy.start()
    copies = []
    for chunk in range(chunks):
        for owner in range(chunk * many, (chunk + 1) * many):
            block = jnp.stack([in_ref[owner, pl.ds(filt * group, group), :] for filt in range(filts)], axis=0)
            for at, row in enumerate(turn_blocks(block)):
                sig_ref[at, pl.ds(owner * filts, filts), :] = row
        rows = pl.ds(chunk * span, span)
        copies.append(pltpu.make_async_copy(sig_ref.at[:, rows, :], sig_hbm.at[:, rows, :], sems.at[chunk]))
        copies[-1].start()
    for copy in copies:
        copy.wait()
    fil_copy.wait()


def pack_rows(plan, owners, sizes, cot, sig, fil):
    _, _, group, filts, _ = plan
    channels, local = cot.shape
    outs = [jax.ShapeDtypeStruct((owners, rows, local), f32) for rows in sizes]
    if (group, filts) != (8, 8):
        return vmem_call(functools.partial(pack_kernel, plan, owners), outs, (cot, sig, fil), "pack_rows", 1e6)
    chunks = math.gcd(owners, 4)
    grouped = (group, channels // group, local)
    return pl.pallas_call(
        functools.partial(pack_copied_kernel, plan, owners, chunks),
        out_shape=outs,
        in_specs=[pl.BlockSpec(memory_space=pl.ANY)] * 3,
        out_specs=[pl.BlockSpec(memory_space=pltpu.VMEM)] * 2,
        scratch_shapes=[pltpu.VMEM(grouped, f32)] * 2
        + [pltpu.SemaphoreType.DMA((2, chunks)), pltpu.SemaphoreType.DMA],
        compiler_params=pltpu.CompilerParams(vmem_limit_bytes=61 << 20),
        cost_estimate=pl.CostEstimate(flops=0, bytes_accessed=16 * cot.size, transcendentals=0),
        name="pack_rows",
    )(cot.reshape(grouped), sig.reshape(grouped), fil.reshape(owners, filts, local))


def unpack_rows(plan, owners, value):
    _, _, group, filts, _ = plan
    count, local = owners * filts, value.shape[2]
    channels = group * count
    if (group, filts) != (8, 8):
        outs = [jax.ShapeDtypeStruct((channels, local), f32), jax.ShapeDtypeStruct((count, local), f32)]
        return vmem_call(functools.partial(unpack_kernel, plan, owners), outs, (value,), "unpack_rows", 1e6)
    chunks = math.gcd(owners, 4)
    grouped = (group, count, local)
    dsig, dfil = pl.pallas_call(
        functools.partial(unpack_copied_kernel, plan, owners, chunks),
        out_shape=[jax.ShapeDtypeStruct(grouped, f32), jax.ShapeDtypeStruct((owners, filts, local), f32)],
        in_specs=[pl.BlockSpec(memory_space=pltpu.VMEM)],
        out_specs=[pl.BlockSpec(memory_space=pl.ANY)] * 2,
        scratch_shapes=[pltpu.VMEM(grouped, f32), pltpu.SemaphoreType.DMA((chunks,)), pltpu.SemaphoreType.DMA],
        compiler_params=pltpu.CompilerParams(vmem_limit_bytes=44 << 20),
        cost_estimate=pl.CostEstimate(flops=0, bytes_accessed=8 * value.size, transcendentals=0),
        name="unpack_rows",
    )(value)
    return dsig.reshape(channels, local), dfil.reshape(count, local)


def body(signal, cotangent, filters):
    ranks, halves = lax.axis_size("ctx"), lax.axis_size("tp")
    channels, local = signal.shape
    count = filters.shape[0]
    both = count % (8 * ranks * halves) == 0
    axes, sources = (("ctx", "tp"), halves) if both else ("ctx", 1)
    owners = ranks * sources
    group, filts = channels // count, count // owners
    early = filts - 1
    plan = (ranks, sources, group, filts, early)

    def exchange(value):
        return lax.all_to_all(value, axes, split_axis=0, concat_axis=0, tiled=True)

    sizes = (2 * early * group + filts, 2 * (filts - early) * group)
    sends = pack_rows(plan, owners, sizes, cotangent, signal, filters)
    first = exchange(sends[0])
    first, late = lax.optimization_barrier((first, sends[1]))
    second = exchange(late)
    grads = call_gradients(plan, 0, early, first, first)
    grads = call_gradients(plan, early, filts, first, second, grads)
    grad_signal, grad_filters = unpack_rows(plan, owners, exchange(grads))
    if not both:
        grad_filters = lax.psum(grad_filters, "tp")
    return grad_signal, grad_filters


def solution(mesh):
    return jax.shard_map(
        body,
        mesh=mesh,
        in_specs=(P("tp", "ctx"), P("tp", "ctx"), P(None, "ctx")),
        out_specs=(P("tp", "ctx"), P(None, "ctx")),
        check_vma=False,
    )
```

```python
import functools
import math

import jax
import jax.numpy as jnp
from jax import lax
from jax.experimental import pallas as pl
from jax.experimental.pallas import tpu as pltpu
from jax.sharding import PartitionSpec as P

f32, bf16 = jnp.float32, jnp.bfloat16
PAIR = 256


def split_two(value):
    high = value.astype(bf16)
    low = (value - high.astype(f32)).astype(bf16)
    return high, low


def rotate_left(value, shift):
    half = value.shape[1] // 2
    if shift == half:
        return jnp.concatenate([value[:, half:], value[:, :half]], axis=1)
    return pltpu.roll(value, value.shape[1] - shift, 1)


def load_blocks(ref, start, blocks, sources, group):
    pieces = []
    for b in range(blocks):
        for s in range(sources):
            pieces.append(ref[b * sources + s, pl.ds(start, group), :])
    even = jnp.concatenate([p for at, p in enumerate(pieces) if at // sources % 2 == 0], axis=0)
    odd = jnp.concatenate([p for at, p in enumerate(pieces) if at // sources % 2 == 1], axis=0)
    return jnp.concatenate([even, odd], axis=1)


def gradients_kernel(plan, data_ref, out_ref, strip_high, strip_low, cot_high, cot_low, weight_ref, prod_ref):
    blocks, sources, group, filts = plan
    local = data_ref.shape[2]
    pairs = blocks // 2
    step_rows = sources * group
    rows_all = pairs * step_rows
    length = blocks * local
    held = cot_high.dtype
    flip = lax.broadcasted_iota(jnp.int32, (local, local), 0) + lax.broadcasted_iota(jnp.int32, (local, local), 1)
    flip = jnp.where(flip == local - 1, 1.0, 0.0).astype(bf16)
    weight_ref[pl.ds(3 * rows_all, 256), :] = jnp.zeros((256, PAIR), held)
    prod_ref[pairs] = jnp.zeros((PAIR, PAIR), f32)
    lane = lax.broadcasted_iota(jnp.int32, (8, PAIR), 1)
    sub = lax.broadcasted_iota(jnp.int32, (8 * pairs, PAIR), 0)
    ahead = lane[:, :128] - sub[:8, :128]

    def one_filter(filt, carry):
        rows = load_blocks(data_ref, filt * group, blocks, sources, group)
        high, low = split_two(rows)
        cot_high[pl.ds(0, rows_all), :] = high.astype(held)
        cot_low[pl.ds(0, rows_all), :] = low.astype(held)
        for at in range(0, rows_all, step_rows):
            for turn_at, part in enumerate((high, low, high)):
                weight_ref[pl.ds(3 * at + turn_at * step_rows, step_rows), :] = part[at : at + step_rows].astype(held)

        lags = [data_ref[b * sources, pl.ds(2 * filts * group + filt, 1), :] for b in reversed(range(blocks))]
        high, low = split_two(jnp.concatenate(lags, axis=0))
        back = jnp.dot(high, flip, preferred_element_type=f32) + jnp.dot(low, flip, preferred_element_type=f32)
        back = [jnp.broadcast_to(back[b : b + 1, :], (8, local)) for b in range(blocks)]
        back = jnp.concatenate(back + [jnp.zeros((8, PAIR), f32)], axis=1)
        skewed = pltpu.roll(back, 1, 1, stride=1, stride_axis=0)
        two = jnp.concatenate([skewed, pltpu.roll(skewed, 8, 1)], axis=0)
        high, low = split_two(two)
        high, low = high.astype(f32), low.astype(f32)
        for step in range(local // 16):
            strip_high[pl.ds(16 * step, 16), :] = pltpu.roll(high, 16 * step, 1).astype(bf16)
            strip_low[pl.ds(16 * step, 16), :] = pltpu.roll(low, 16 * step, 1).astype(bf16)

        sig = load_blocks(data_ref, (filts + filt) * group, blocks, sources, group)
        sig_high = sig.astype(bf16).astype(f32)
        sig_low = sig - sig_high
        stacked = []
        for at in range(0, rows_all, step_rows):
            stacked += [part[at : at + step_rows] for part in (sig_high, sig_high, sig_low)]
        turned = jnp.concatenate(stacked, axis=0).T.astype(bf16)
        for gap in range(pairs):
            deep = min(-(-3 * (rows_all - gap * step_rows) // 256) * 256, 3 * rows_all)
            weights = weight_ref[pl.ds(3 * gap * step_rows, deep), :].astype(bf16)
            prod_ref[gap] = jnp.dot(turned[:, :deep], weights, preferred_element_type=f32)

        total = None
        for gap in range(pairs):
            kept = rows_all - gap * step_rows
            high = cot_high[pl.ds(gap * step_rows, kept), :].astype(bf16)
            low = cot_low[pl.ds(gap * step_rows, kept), :].astype(bf16)
            at = length - gap * PAIR
            t_high = jnp.concatenate([strip_high[:, pl.ds(at, PAIR)], strip_high[:, pl.ds(at - local, PAIR)]], axis=0)
            t_low = jnp.concatenate([strip_low[:, pl.ds(at, PAIR)], strip_low[:, pl.ds(at - local, PAIR)]], axis=0)
            both = jnp.dot(jnp.concatenate([high, low], axis=0), t_high, preferred_element_type=f32)
            part = both[:kept] + both[kept:] + jnp.dot(high, t_low, preferred_element_type=f32)
            if total is None:
                total = part
            else:
                part = jnp.concatenate([part, jnp.zeros((gap * step_rows, PAIR), f32)], axis=0)
                total = total + part
        for b in range(blocks):
            for s in range(sources):
                at = b // 2 * step_rows + s * group
                piece = total[at : at + group, b % 2 * local : (b % 2 + 1) * local]
                out_ref[b * sources + s, pl.ds(filt * group, group), :] = piece

        def leaf(gap, step):
            near, far = pl.ds(8 * step, 8), pl.ds(8 * step + 128, 8)
            left, right = pl.ds(0, 128), pl.ds(128, 128)
            valid = ahead >= 8 * step
            first = jnp.where(valid, prod_ref[gap, near, left], prod_ref[gap + 1, near, left])
            second = jnp.where(valid, prod_ref[gap, far, right], prod_ref[gap + 1, far, right])
            return jnp.concatenate([first + second, prod_ref[gap, near, right] + prod_ref[gap + 1, far, left]], axis=1)

        lagged = []
        for gap in range(pairs):
            summed = leaf(gap, 0)
            for step in range(1, PAIR // 16):
                summed = summed + rotate_left(leaf(gap, step), 8 * step)
            lagged.append(summed)
        lagged = jnp.concatenate(lagged, axis=0)
        for bit in (1, 2, 4):
            lagged = jnp.where((sub & bit) != 0, rotate_left(lagged, bit), lagged)
        lagged = jnp.sum(lagged.reshape(pairs, 8, PAIR), axis=1)
        for gap in range(pairs):
            for s in range(sources):
                row = pl.ds(filts * group + filt, 1)
                out_ref[2 * gap * sources + s, row, :] = lagged[gap : gap + 1, :local]
                out_ref[(2 * gap + 1) * sources + s, row, :] = lagged[gap : gap + 1, local:]
        return carry

    lax.fori_loop(0, filts, one_filter, 0)


def vmem_call(kernel, outs, args, name, flops, scratch=()):
    return pl.pallas_call(
        kernel,
        out_shape=outs,
        in_specs=[pl.BlockSpec(memory_space=pltpu.VMEM)] * len(args),
        out_specs=jax.tree.map(lambda _: pl.BlockSpec(memory_space=pltpu.VMEM), outs),
        scratch_shapes=list(scratch),
        compiler_params=pltpu.CompilerParams(vmem_limit_bytes=44 << 20),
        cost_estimate=pl.CostEstimate(
            flops=int(flops), bytes_accessed=sum(4 * a.size for a in args), transcendentals=0
        ),
        name=name,
    )(*args)


def call_gradients(plan, data):
    blocks, sources, group, filts = plan
    local = data.shape[2]
    rows = blocks * sources * group
    held = bf16 if sources * group % 16 == 0 else f32
    scratch = (
        [pltpu.VMEM((local, blocks * local + PAIR), bf16)] * 2
        + [pltpu.VMEM((rows // 2, PAIR), held)] * 2
        + [pltpu.VMEM((3 * rows // 2 + 256, PAIR), held), pltpu.VMEM((blocks // 2 + 1, PAIR, PAIR), f32)]
    )
    outs = jax.ShapeDtypeStruct((blocks * sources, filts * group + filts, local), f32)
    kernel = functools.partial(gradients_kernel, plan)
    return vmem_call(kernel, outs, (data,), "gradients", filts * 3e9, scratch)


def pack_kernel(plan, owners, cot_ref, sig_ref, fil_ref, out_ref):
    _, _, group, filts = plan
    count = owners * filts

    def one_owner(owner, carry):
        for filt in range(filts):
            for part, source in enumerate((cot_ref, sig_ref)):
                rows = source[pl.ds(owner * filts + filt, group, stride=count), :]
                out_ref[owner, pl.ds((part * filts + filt) * group, group), :] = rows
        out_ref[owner, pl.ds(2 * filts * group, filts), :] = fil_ref[pl.ds(owner * filts, filts), :]
        return carry

    lax.fori_loop(0, owners, one_owner, 0)


def unpack_kernel(plan, owners, in_ref, sig_ref, fil_ref):
    _, _, group, filts = plan
    count = owners * filts

    def one_owner(owner, carry):
        for filt in range(filts):
            sig_ref[pl.ds(owner * filts + filt, group, stride=count), :] = in_ref[owner, pl.ds(filt * group, group), :]
        fil_ref[pl.ds(owner * filts, filts), :] = in_ref[owner, pl.ds(filts * group, filts), :]
        return carry

    lax.fori_loop(0, owners, one_owner, 0)


def turn_blocks(value):
    rows = [value[at] for at in range(8)]
    sub = lax.broadcasted_iota(jnp.int32, rows[0].shape, 0)
    for bit in (1, 2, 4):
        clear = (sub & bit) == 0
        turned = list(rows)
        for at in range(8):
            if at & bit == 0:
                turned[at] = jnp.where(clear, rows[at], pltpu.roll(rows[at + bit], bit, 0))
                turned[at + bit] = jnp.where(clear, pltpu.roll(rows[at], 8 - bit, 0), rows[at + bit])
        rows = turned
    return rows


def pack_copied_kernel(plan, owners, chunks, cot_hbm, sig_hbm, fil_hbm, out_ref, cot_ref, sig_ref, sems, fil_sem):
    _, _, group, filts = plan
    many = owners // chunks
    span = many * filts
    copies = []
    for chunk in range(chunks):
        for part, (source, target) in enumerate(((cot_hbm, cot_ref), (sig_hbm, sig_ref))):
            rows = pl.ds(chunk * span, span)
            copies.append(pltpu.make_async_copy(source.at[:, rows, :], target.at[:, rows, :], sems.at[part, chunk]))
            copies[-1].start()
    fil_copy = pltpu.make_async_copy(fil_hbm, out_ref.at[:, pl.ds(2 * filts * group, filts), :], fil_sem)
    fil_copy.start()
    for chunk in range(chunks):
        for part, source in enumerate((cot_ref, sig_ref)):
            copies[2 * chunk + part].wait()
            for owner in range(chunk * many, (chunk + 1) * many):
                rows = turn_blocks(source[:, pl.ds(owner * filts, filts), :])
                for filt in range(filts):
                    out_ref[owner, pl.ds((part * filts + filt) * group, group), :] = rows[filt]
    fil_copy.wait()


def unpack_copied_kernel(plan, owners, chunks, in_ref, sig_hbm, fil_hbm, sig_ref, sems, fil_sem):
    _, _, group, filts = plan
    many = owners // chunks
    span = many * filts
    fil_copy = pltpu.make_async_copy(in_ref.at[:, pl.ds(filts * group, filts), :], fil_hbm, fil_sem)
    fil_copy.start()
    copies = []
    for chunk in range(chunks):
        for owner in range(chunk * many, (chunk + 1) * many):
            block = jnp.stack([in_ref[owner, pl.ds(filt * group, group), :] for filt in range(filts)], axis=0)
            for at, row in enumerate(turn_blocks(block)):
                sig_ref[at, pl.ds(owner * filts, filts), :] = row
        rows = pl.ds(chunk * span, span)
        copies.append(pltpu.make_async_copy(sig_ref.at[:, rows, :], sig_hbm.at[:, rows, :], sems.at[chunk]))
        copies[-1].start()
    for copy in copies:
        copy.wait()
    fil_copy.wait()


def pack_rows(plan, owners, cot, sig, fil):
    _, _, group, filts = plan
    channels, local = cot.shape
    out = jax.ShapeDtypeStruct((owners, 2 * filts * group + filts, local), f32)
    if (group, filts) != (8, 8):
        return vmem_call(functools.partial(pack_kernel, plan, owners), out, (cot, sig, fil), "pack_rows", 1e6)
    chunks = math.gcd(owners, 4)
    grouped = (group, channels // group, local)
    return pl.pallas_call(
        functools.partial(pack_copied_kernel, plan, owners, chunks),
        out_shape=out,
        in_specs=[pl.BlockSpec(memory_space=pl.ANY)] * 3,
        out_specs=pl.BlockSpec(memory_space=pltpu.VMEM),
        scratch_shapes=[pltpu.VMEM(grouped, f32)] * 2
        + [pltpu.SemaphoreType.DMA((2, chunks)), pltpu.SemaphoreType.DMA],
        compiler_params=pltpu.CompilerParams(vmem_limit_bytes=61 << 20),
        cost_estimate=pl.CostEstimate(flops=0, bytes_accessed=16 * cot.size, transcendentals=0),
        name="pack_rows",
    )(cot.reshape(grouped), sig.reshape(grouped), fil.reshape(owners, filts, local))


def unpack_rows(plan, owners, value):
    _, _, group, filts = plan
    count, local = owners * filts, value.shape[2]
    channels = group * count
    if (group, filts) != (8, 8):
        outs = [jax.ShapeDtypeStruct((channels, local), f32), jax.ShapeDtypeStruct((count, local), f32)]
        return vmem_call(functools.partial(unpack_kernel, plan, owners), outs, (value,), "unpack_rows", 1e6)
    chunks = math.gcd(owners, 4)
    grouped = (group, count, local)
    dsig, dfil = pl.pallas_call(
        functools.partial(unpack_copied_kernel, plan, owners, chunks),
        out_shape=[jax.ShapeDtypeStruct(grouped, f32), jax.ShapeDtypeStruct((owners, filts, local), f32)],
        in_specs=[pl.BlockSpec(memory_space=pltpu.VMEM)],
        out_specs=[pl.BlockSpec(memory_space=pl.ANY)] * 2,
        scratch_shapes=[pltpu.VMEM(grouped, f32), pltpu.SemaphoreType.DMA((chunks,)), pltpu.SemaphoreType.DMA],
        compiler_params=pltpu.CompilerParams(vmem_limit_bytes=44 << 20),
        cost_estimate=pl.CostEstimate(flops=0, bytes_accessed=8 * value.size, transcendentals=0),
        name="unpack_rows",
    )(value)
    return dsig.reshape(channels, local), dfil.reshape(count, local)


def body(signal, cotangent, filters):
    ranks, halves = lax.axis_size("ctx"), lax.axis_size("tp")
    channels, local = signal.shape
    count = filters.shape[0]
    both = count % (8 * ranks * halves) == 0
    axes, sources = (("ctx", "tp"), halves) if both else ("ctx", 1)
    owners = ranks * sources
    group, filts = channels // count, count // owners
    plan = (ranks, sources, group, filts)

    def exchange(value):
        return lax.all_to_all(value, axes, split_axis=0, concat_axis=0, tiled=True)

    data = exchange(pack_rows(plan, owners, cotangent, signal, filters))
    grad_signal, grad_filters = unpack_rows(plan, owners, exchange(call_gradients(plan, data)))
    if not both:
        grad_filters = lax.psum(grad_filters, "tp")
    return grad_signal, grad_filters


def solution(mesh):
    return jax.shard_map(
        body,
        mesh=mesh,
        in_specs=(P("tp", "ctx"), P("tp", "ctx"), P(None, "ctx")),
        out_specs=(P("tp", "ctx"), P(None, "ctx")),
        check_vma=False,
    )
```

```python
import functools
import math

import jax
import jax.numpy as jnp
from jax import lax
from jax.experimental import pallas as pl
from jax.experimental.pallas import tpu as pltpu
from jax.sharding import PartitionSpec as P

f32, bf16 = jnp.float32, jnp.bfloat16
PAIR = 256


def split_two(value):
    high = value.astype(bf16)
    low = (value - high.astype(f32)).astype(bf16)
    return high, low


def rotate_left(value, shift):
    half = value.shape[1] // 2
    if shift == half:
        return jnp.concatenate([value[:, half:], value[:, :half]], axis=1)
    return pltpu.roll(value, value.shape[1] - shift, 1)


def load_blocks(ref, start, blocks, sources, group):
    pieces = []
    for b in range(blocks):
        for s in range(sources):
            pieces.append(ref[b * sources + s, pl.ds(start, group), :])
    even = jnp.concatenate([p for at, p in enumerate(pieces) if at // sources % 2 == 0], axis=0)
    odd = jnp.concatenate([p for at, p in enumerate(pieces) if at // sources % 2 == 1], axis=0)
    return jnp.concatenate([even, odd], axis=1)


def gradients_kernel(plan, data_ref, out_ref, lag_ref, *scratch):
    slots = [scratch[at : at + 6] for at in range(0, len(scratch), 6)]
    blocks, sources, group, filts = plan
    local = data_ref.shape[2]
    pairs = blocks // 2
    step_rows = sources * group
    rows_all = pairs * step_rows
    length = blocks * local
    held = slots[0][2].dtype
    flip = lax.broadcasted_iota(jnp.int32, (local, local), 0) + lax.broadcasted_iota(jnp.int32, (local, local), 1)
    flip = jnp.where(flip == local - 1, 1.0, 0.0).astype(bf16)
    for *_, weight_ref, prod_ref in slots:
        weight_ref[pl.ds(3 * rows_all, 256), :] = jnp.zeros((256, PAIR), held)
        prod_ref[pairs] = jnp.zeros((PAIR, PAIR), f32)
    lane = lax.broadcasted_iota(jnp.int32, (8, PAIR), 1)
    sub = lax.broadcasted_iota(jnp.int32, (8 * pairs, PAIR), 0)
    ahead = lane[:, :128] - sub[:8, :128]

    for b in range(blocks):
        high, low = split_two(data_ref[b * sources, pl.ds(2 * filts * group, filts), :])
        lag_ref[b] = jnp.dot(high, flip, preferred_element_type=f32) + jnp.dot(low, flip, preferred_element_type=f32)

    def one_filter(filt, slot):
        strip_high, strip_low, cot_high, cot_low, weight_ref, prod_ref = slots[slot]
        rows = load_blocks(data_ref, filt * group, blocks, sources, group)
        high, low = split_two(rows)
        cot_high[pl.ds(0, rows_all), :] = high.astype(held)
        cot_low[pl.ds(0, rows_all), :] = low.astype(held)
        for at in range(0, rows_all, step_rows):
            for turn_at, part in enumerate((high, low, high)):
                weight_ref[pl.ds(3 * at + turn_at * step_rows, step_rows), :] = part[at : at + step_rows].astype(held)

        back = [jnp.broadcast_to(lag_ref[b, pl.ds(filt, 1), :], (8, local)) for b in reversed(range(blocks))]
        back = jnp.concatenate(back + [jnp.zeros((8, PAIR), f32)], axis=1)
        skewed = pltpu.roll(back, 1, 1, stride=1, stride_axis=0)
        two = jnp.concatenate([skewed, pltpu.roll(skewed, 8, 1)], axis=0)
        high, low = split_two(two)
        high, low = high.astype(f32), low.astype(f32)
        for step in range(local // 16):
            strip_high[pl.ds(16 * step, 16), :] = pltpu.roll(high, 16 * step, 1).astype(bf16)
            strip_low[pl.ds(16 * step, 16), :] = pltpu.roll(low, 16 * step, 1).astype(bf16)

        sig = load_blocks(data_ref, (filts + filt) * group, blocks, sources, group)
        sig_high = sig.astype(bf16).astype(f32)
        sig_low = sig - sig_high
        stacked = []
        for at in range(0, rows_all, step_rows):
            stacked += [part[at : at + step_rows] for part in (sig_high, sig_high, sig_low)]
        turned = jnp.concatenate(stacked, axis=0).T.astype(bf16)
        for gap in range(pairs):
            deep = min(-(-3 * (rows_all - gap * step_rows) // 256) * 256, 3 * rows_all)
            weights = weight_ref[pl.ds(3 * gap * step_rows, deep), :].astype(bf16)
            prod_ref[gap] = jnp.dot(turned[:, :deep], weights, preferred_element_type=f32)

        total = None
        for gap in range(pairs):
            kept = rows_all - gap * step_rows
            high = cot_high[pl.ds(gap * step_rows, kept), :].astype(bf16)
            low = cot_low[pl.ds(gap * step_rows, kept), :].astype(bf16)
            at = length - gap * PAIR
            t_high = jnp.concatenate([strip_high[:, pl.ds(at, PAIR)], strip_high[:, pl.ds(at - local, PAIR)]], axis=0)
            t_low = jnp.concatenate([strip_low[:, pl.ds(at, PAIR)], strip_low[:, pl.ds(at - local, PAIR)]], axis=0)
            both = jnp.dot(jnp.concatenate([high, low], axis=0), t_high, preferred_element_type=f32)
            part = both[:kept] + both[kept:] + jnp.dot(high, t_low, preferred_element_type=f32)
            if total is None:
                total = part
            else:
                part = jnp.concatenate([part, jnp.zeros((gap * step_rows, PAIR), f32)], axis=0)
                total = total + part
        for b in range(blocks):
            for s in range(sources):
                at = b // 2 * step_rows + s * group
                piece = total[at : at + group, b % 2 * local : (b % 2 + 1) * local]
                out_ref[b * sources + s, pl.ds(filt * group, group), :] = piece

        def leaf(gap, step):
            near, far = pl.ds(8 * step, 8), pl.ds(8 * step + 128, 8)
            left, right = pl.ds(0, 128), pl.ds(128, 128)
            valid = ahead >= 8 * step
            first = jnp.where(valid, prod_ref[gap, near, left], prod_ref[gap + 1, near, left])
            second = jnp.where(valid, prod_ref[gap, far, right], prod_ref[gap + 1, far, right])
            return jnp.concatenate([first + second, prod_ref[gap, near, right] + prod_ref[gap + 1, far, left]], axis=1)

        lagged = []
        for gap in range(pairs):
            summed = leaf(gap, 0)
            for step in range(1, PAIR // 16):
                summed = summed + rotate_left(leaf(gap, step), 8 * step)
            lagged.append(summed)
        lagged = jnp.concatenate(lagged, axis=0)
        for bit in (1, 2, 4):
            lagged = jnp.where((sub & bit) != 0, rotate_left(lagged, bit), lagged)
        lagged = jnp.sum(lagged.reshape(pairs, 8, PAIR), axis=1)
        for gap in range(pairs):
            for s in range(sources):
                row = pl.ds(filts * group + filt, 1)
                out_ref[2 * gap * sources + s, row, :] = lagged[gap : gap + 1, :local]
                out_ref[(2 * gap + 1) * sources + s, row, :] = lagged[gap : gap + 1, local:]

    def some_filters(turn, carry):
        for slot in range(len(slots)):
            one_filter(turn * len(slots) + slot, slot)
        return carry

    lax.fori_loop(0, filts // len(slots), some_filters, 0)


def vmem_call(kernel, outs, args, name, flops, scratch=()):
    return pl.pallas_call(
        kernel,
        out_shape=outs,
        in_specs=[pl.BlockSpec(memory_space=pltpu.VMEM)] * len(args),
        out_specs=jax.tree.map(lambda _: pl.BlockSpec(memory_space=pltpu.VMEM), outs),
        scratch_shapes=list(scratch),
        compiler_params=pltpu.CompilerParams(vmem_limit_bytes=44 << 20),
        cost_estimate=pl.CostEstimate(
            flops=int(flops), bytes_accessed=sum(4 * a.size for a in args), transcendentals=0
        ),
        name=name,
    )(*args)


def call_gradients(plan, data):
    blocks, sources, group, filts = plan
    local = data.shape[2]
    rows = blocks * sources * group
    held = bf16 if sources * group % 16 == 0 else f32
    scratch = (
        [pltpu.VMEM((local, blocks * local + PAIR), bf16)] * 2
        + [pltpu.VMEM((rows // 2, PAIR), held)] * 2
        + [pltpu.VMEM((3 * rows // 2 + 256, PAIR), held), pltpu.VMEM((blocks // 2 + 1, PAIR, PAIR), f32)]
    )
    scratch = [pltpu.VMEM((blocks, filts, local), f32)] + scratch * 2
    outs = jax.ShapeDtypeStruct((blocks * sources, filts * group + filts, local), f32)
    kernel = functools.partial(gradients_kernel, plan)
    return vmem_call(kernel, outs, (data,), "gradients", filts * 3e9, scratch)


def pack_kernel(plan, owners, cot_ref, sig_ref, fil_ref, out_ref):
    _, _, group, filts = plan
    count = owners * filts

    def one_owner(owner, carry):
        for filt in range(filts):
            for part, source in enumerate((cot_ref, sig_ref)):
                rows = source[pl.ds(owner * filts + filt, group, stride=count), :]
                out_ref[owner, pl.ds((part * filts + filt) * group, group), :] = rows
        out_ref[owner, pl.ds(2 * filts * group, filts), :] = fil_ref[pl.ds(owner * filts, filts), :]
        return carry

    lax.fori_loop(0, owners, one_owner, 0)


def unpack_kernel(plan, owners, in_ref, sig_ref, fil_ref):
    _, _, group, filts = plan
    count = owners * filts

    def one_owner(owner, carry):
        for filt in range(filts):
            sig_ref[pl.ds(owner * filts + filt, group, stride=count), :] = in_ref[owner, pl.ds(filt * group, group), :]
        fil_ref[pl.ds(owner * filts, filts), :] = in_ref[owner, pl.ds(filts * group, filts), :]
        return carry

    lax.fori_loop(0, owners, one_owner, 0)


def turn_blocks(value):
    rows = [value[at] for at in range(8)]
    sub = lax.broadcasted_iota(jnp.int32, rows[0].shape, 0)
    for bit in (1, 2, 4):
        clear = (sub & bit) == 0
        turned = list(rows)
        for at in range(8):
            if at & bit == 0:
                turned[at] = jnp.where(clear, rows[at], pltpu.roll(rows[at + bit], bit, 0))
                turned[at + bit] = jnp.where(clear, pltpu.roll(rows[at], 8 - bit, 0), rows[at + bit])
        rows = turned
    return rows


def pack_copied_kernel(plan, owners, chunks, cot_hbm, sig_hbm, fil_hbm, out_ref, cot_ref, sig_ref, sems, fil_sem):
    _, _, group, filts = plan
    many = owners // chunks
    span = many * filts
    copies = []
    for chunk in range(chunks):
        for part, (source, target) in enumerate(((cot_hbm, cot_ref), (sig_hbm, sig_ref))):
            rows = pl.ds(chunk * span, span)
            copies.append(pltpu.make_async_copy(source.at[:, rows, :], target.at[:, rows, :], sems.at[part, chunk]))
            copies[-1].start()
    fil_copy = pltpu.make_async_copy(fil_hbm, out_ref.at[:, pl.ds(2 * filts * group, filts), :], fil_sem)
    fil_copy.start()
    for chunk in range(chunks):
        for part, source in enumerate((cot_ref, sig_ref)):
            copies[2 * chunk + part].wait()
            for owner in range(chunk * many, (chunk + 1) * many):
                rows = turn_blocks(source[:, pl.ds(owner * filts, filts), :])
                for filt in range(filts):
                    out_ref[owner, pl.ds((part * filts + filt) * group, group), :] = rows[filt]
    fil_copy.wait()


def unpack_copied_kernel(plan, owners, chunks, in_ref, sig_hbm, fil_hbm, sig_ref, sems, fil_sem):
    _, _, group, filts = plan
    many = owners // chunks
    span = many * filts
    fil_copy = pltpu.make_async_copy(in_ref.at[:, pl.ds(filts * group, filts), :], fil_hbm, fil_sem)
    fil_copy.start()
    copies = []
    for chunk in range(chunks):
        for owner in range(chunk * many, (chunk + 1) * many):
            block = jnp.stack([in_ref[owner, pl.ds(filt * group, group), :] for filt in range(filts)], axis=0)
            for at, row in enumerate(turn_blocks(block)):
                sig_ref[at, pl.ds(owner * filts, filts), :] = row
        rows = pl.ds(chunk * span, span)
        copies.append(pltpu.make_async_copy(sig_ref.at[:, rows, :], sig_hbm.at[:, rows, :], sems.at[chunk]))
        copies[-1].start()
    for copy in copies:
        copy.wait()
    fil_copy.wait()


def pack_rows(plan, owners, cot, sig, fil):
    _, _, group, filts = plan
    channels, local = cot.shape
    out = jax.ShapeDtypeStruct((owners, 2 * filts * group + filts, local), f32)
    if (group, filts) != (8, 8):
        return vmem_call(functools.partial(pack_kernel, plan, owners), out, (cot, sig, fil), "pack_rows", 1e6)
    chunks = math.gcd(owners, 4)
    grouped = (group, channels // group, local)
    return pl.pallas_call(
        functools.partial(pack_copied_kernel, plan, owners, chunks),
        out_shape=out,
        in_specs=[pl.BlockSpec(memory_space=pl.ANY)] * 3,
        out_specs=pl.BlockSpec(memory_space=pltpu.VMEM),
        scratch_shapes=[pltpu.VMEM(grouped, f32)] * 2
        + [pltpu.SemaphoreType.DMA((2, chunks)), pltpu.SemaphoreType.DMA],
        compiler_params=pltpu.CompilerParams(vmem_limit_bytes=44 << 20),
        cost_estimate=pl.CostEstimate(flops=0, bytes_accessed=16 * cot.size, transcendentals=0),
        name="pack_rows",
    )(*[pltpu.with_memory_space_constraint(x, pltpu.HBM) for x in (cot.reshape(grouped), sig.reshape(grouped), fil.reshape(owners, filts, local))])


def unpack_rows(plan, owners, value):
    _, _, group, filts = plan
    count, local = owners * filts, value.shape[2]
    channels = group * count
    if (group, filts) != (8, 8):
        outs = [jax.ShapeDtypeStruct((channels, local), f32), jax.ShapeDtypeStruct((count, local), f32)]
        return vmem_call(functools.partial(unpack_kernel, plan, owners), outs, (value,), "unpack_rows", 1e6)
    chunks = math.gcd(owners, 4)
    grouped = (group, count, local)
    dsig, dfil = pl.pallas_call(
        functools.partial(unpack_copied_kernel, plan, owners, chunks),
        out_shape=[jax.ShapeDtypeStruct(grouped, f32), jax.ShapeDtypeStruct((owners, filts, local), f32)],
        in_specs=[pl.BlockSpec(memory_space=pltpu.VMEM)],
        out_specs=[pl.BlockSpec(memory_space=pl.ANY)] * 2,
        scratch_shapes=[pltpu.VMEM(grouped, f32), pltpu.SemaphoreType.DMA((chunks,)), pltpu.SemaphoreType.DMA],
        compiler_params=pltpu.CompilerParams(vmem_limit_bytes=44 << 20),
        cost_estimate=pl.CostEstimate(flops=0, bytes_accessed=8 * value.size, transcendentals=0),
        name="unpack_rows",
    )(value)
    return dsig.reshape(channels, local), dfil.reshape(count, local)


def body(signal, cotangent, filters):
    ranks, halves = lax.axis_size("ctx"), lax.axis_size("tp")
    channels, local = signal.shape
    count = filters.shape[0]
    both = count % (8 * ranks * halves) == 0
    axes, sources = (("ctx", "tp"), halves) if both else ("ctx", 1)
    owners = ranks * sources
    group, filts = channels // count, count // owners
    plan = (ranks, sources, group, filts)

    def exchange(value):
        return lax.all_to_all(value, axes, split_axis=0, concat_axis=0, tiled=True)

    data = exchange(pack_rows(plan, owners, cotangent, signal, filters))
    grad_signal, grad_filters = unpack_rows(plan, owners, exchange(call_gradients(plan, data)))
    if not both:
        grad_filters = lax.psum(grad_filters, "tp")
    return grad_signal, grad_filters


def solution(mesh):
    return jax.shard_map(
        body,
        mesh=mesh,
        in_specs=(P("tp", "ctx"), P("tp", "ctx"), P(None, "ctx")),
        out_specs=(P("tp", "ctx"), P(None, "ctx")),
        check_vma=False,
    )
```

```python
import functools
import math

import jax
import jax.numpy as jnp
from jax import lax
from jax.experimental import pallas as pl
from jax.experimental.pallas import tpu as pltpu
from jax.sharding import PartitionSpec as P

f32, bf16 = jnp.float32, jnp.bfloat16
PAIR = 256


def split_two(value):
    high = value.astype(bf16)
    low = (value - high.astype(f32)).astype(bf16)
    return high, low


def rotate_left(value, shift):
    half = value.shape[1] // 2
    if shift == half:
        return jnp.concatenate([value[:, half:], value[:, :half]], axis=1)
    return pltpu.roll(value, value.shape[1] - shift, 1)


def load_blocks(ref, start, blocks, sources, group):
    pieces = []
    for b in range(blocks):
        for s in range(sources):
            pieces.append(ref[b * sources + s, pl.ds(start, group), :])
    even = jnp.concatenate([p for at, p in enumerate(pieces) if at // sources % 2 == 0], axis=0)
    odd = jnp.concatenate([p for at, p in enumerate(pieces) if at // sources % 2 == 1], axis=0)
    return jnp.concatenate([even, odd], axis=1)


def gradients_kernel(plan, data_ref, out_ref, lag_ref, *scratch):
    slots = [scratch[at : at + 6] for at in range(0, len(scratch), 6)]
    blocks, sources, group, filts = plan
    local = data_ref.shape[2]
    pairs = blocks // 2
    step_rows = sources * group
    rows_all = pairs * step_rows
    length = blocks * local
    held = slots[0][2].dtype
    flip = lax.broadcasted_iota(jnp.int32, (local, local), 0) + lax.broadcasted_iota(jnp.int32, (local, local), 1)
    flip = jnp.where(flip == local - 1, 1.0, 0.0).astype(bf16)
    for *_, weight_ref, prod_ref in slots:
        weight_ref[pl.ds(3 * rows_all, 256), :] = jnp.zeros((256, PAIR), held)
        prod_ref[pairs] = jnp.zeros((PAIR, PAIR), f32)
    lane = lax.broadcasted_iota(jnp.int32, (8, PAIR), 1)
    sub = lax.broadcasted_iota(jnp.int32, (8 * pairs, PAIR), 0)
    ahead = lane[:, :128] - sub[:8, :128]

    for b in range(blocks):
        high, low = split_two(data_ref[b * sources, pl.ds(2 * filts * group, filts), :])
        lag_ref[b] = jnp.dot(high, flip, preferred_element_type=f32) + jnp.dot(low, flip, preferred_element_type=f32)

    def one_filter(filt, slot):
        strip_high, strip_low, cot_high, cot_low, weight_ref, prod_ref = slots[slot]
        rows = load_blocks(data_ref, filt * group, blocks, sources, group)
        high, low = split_two(rows)
        cot_high[pl.ds(0, rows_all), :] = high.astype(held)
        cot_low[pl.ds(0, rows_all), :] = low.astype(held)
        for at in range(0, rows_all, step_rows):
            for turn_at, part in enumerate((high, low, high)):
                weight_ref[pl.ds(3 * at + turn_at * step_rows, step_rows), :] = part[at : at + step_rows].astype(held)

        back = [jnp.broadcast_to(lag_ref[b, pl.ds(filt, 1), :], (8, local)) for b in reversed(range(blocks))]
        back = jnp.concatenate(back + [jnp.zeros((8, PAIR), f32)], axis=1)
        skewed = pltpu.roll(back, 1, 1, stride=1, stride_axis=0)
        two = jnp.concatenate([skewed, pltpu.roll(skewed, 8, 1)], axis=0)
        high, low = split_two(two)
        high, low = high.astype(f32), low.astype(f32)
        for step in range(local // 16):
            strip_high[pl.ds(16 * step, 16), :] = pltpu.roll(high, 16 * step, 1).astype(bf16)
            strip_low[pl.ds(16 * step, 16), :] = pltpu.roll(low, 16 * step, 1).astype(bf16)

        sig = load_blocks(data_ref, (filts + filt) * group, blocks, sources, group)
        sig_high = sig.astype(bf16).astype(f32)
        sig_low = sig - sig_high
        stacked = []
        for at in range(0, rows_all, step_rows):
            stacked += [part[at : at + step_rows] for part in (sig_high, sig_high, sig_low)]
        turned = jnp.concatenate(stacked, axis=0).T.astype(bf16)
        for gap in range(pairs):
            deep = min(-(-3 * (rows_all - gap * step_rows) // 128) * 128, 3 * rows_all)
            weights = weight_ref[pl.ds(3 * gap * step_rows, deep), :].astype(bf16)
            prod_ref[gap] = jnp.dot(turned[:, :deep], weights, preferred_element_type=f32)

        total = None
        for gap in range(pairs):
            kept = rows_all - gap * step_rows
            high = cot_high[pl.ds(gap * step_rows, kept), :].astype(bf16)
            low = cot_low[pl.ds(gap * step_rows, kept), :].astype(bf16)
            at = length - gap * PAIR
            t_high = jnp.concatenate([strip_high[:, pl.ds(at, PAIR)], strip_high[:, pl.ds(at - local, PAIR)]], axis=0)
            t_low = jnp.concatenate([strip_low[:, pl.ds(at, PAIR)], strip_low[:, pl.ds(at - local, PAIR)]], axis=0)
            both = jnp.dot(jnp.concatenate([high, low], axis=0), t_high, preferred_element_type=f32)
            part = both[:kept] + both[kept:] + jnp.dot(high, t_low, preferred_element_type=f32)
            if total is None:
                total = part
            else:
                part = jnp.concatenate([part, jnp.zeros((gap * step_rows, PAIR), f32)], axis=0)
                total = total + part
        for b in range(blocks):
            for s in range(sources):
                at = b // 2 * step_rows + s * group
                piece = total[at : at + group, b % 2 * local : (b % 2 + 1) * local]
                out_ref[b * sources + s, pl.ds(filt * group, group), :] = piece

        def leaf(gap, step):
            near, far = pl.ds(8 * step, 8), pl.ds(8 * step + 128, 8)
            left, right = pl.ds(0, 128), pl.ds(128, 128)
            valid = ahead >= 8 * step
            first = jnp.where(valid, prod_ref[gap, near, left], prod_ref[gap + 1, near, left])
            second = jnp.where(valid, prod_ref[gap, far, right], prod_ref[gap + 1, far, right])
            return jnp.concatenate([first + second, prod_ref[gap, near, right] + prod_ref[gap + 1, far, left]], axis=1)

        lagged = []
        for gap in range(pairs):
            summed = leaf(gap, 0)
            for step in range(1, PAIR // 16):
                summed = summed + rotate_left(leaf(gap, step), 8 * step)
            lagged.append(summed)
        lagged = jnp.concatenate(lagged, axis=0)
        for bit in (1, 2, 4):
            lagged = jnp.where((sub & bit) != 0, rotate_left(lagged, bit), lagged)
        lagged = jnp.sum(lagged.reshape(pairs, 8, PAIR), axis=1)
        for gap in range(pairs):
            for s in range(sources):
                row = pl.ds(filts * group + filt, 1)
                out_ref[2 * gap * sources + s, row, :] = lagged[gap : gap + 1, :local]
                out_ref[(2 * gap + 1) * sources + s, row, :] = lagged[gap : gap + 1, local:]

    def some_filters(turn, carry):
        for slot in range(len(slots)):
            one_filter(turn * len(slots) + slot, slot)
        return carry

    lax.fori_loop(0, filts // len(slots), some_filters, 0)


def vmem_call(kernel, outs, args, name, flops, scratch=()):
    return pl.pallas_call(
        kernel,
        out_shape=outs,
        in_specs=[pl.BlockSpec(memory_space=pltpu.VMEM)] * len(args),
        out_specs=jax.tree.map(lambda _: pl.BlockSpec(memory_space=pltpu.VMEM), outs),
        scratch_shapes=list(scratch),
        compiler_params=pltpu.CompilerParams(vmem_limit_bytes=44 << 20),
        cost_estimate=pl.CostEstimate(
            flops=int(flops), bytes_accessed=sum(4 * a.size for a in args), transcendentals=0
        ),
        name=name,
    )(*args)


def call_gradients(plan, data):
    blocks, sources, group, filts = plan
    local = data.shape[2]
    rows = blocks * sources * group
    held = bf16 if sources * group % 16 == 0 else f32
    scratch = (
        [pltpu.VMEM((local, blocks * local + PAIR), bf16)] * 2
        + [pltpu.VMEM((rows // 2, PAIR), held)] * 2
        + [pltpu.VMEM((3 * rows // 2 + 256, PAIR), held), pltpu.VMEM((blocks // 2 + 1, PAIR, PAIR), f32)]
    )
    scratch = [pltpu.VMEM((blocks, filts, local), f32)] + scratch * (2 if filts % 2 == 0 else 1)
    outs = jax.ShapeDtypeStruct((blocks * sources, filts * group + filts, local), f32)
    kernel = functools.partial(gradients_kernel, plan)
    return vmem_call(kernel, outs, (data,), "gradients", filts * 3e9, scratch)


def pack_kernel(plan, owners, cot_ref, sig_ref, fil_ref, out_ref):
    _, _, group, filts = plan
    count = owners * filts

    def one_owner(owner, carry):
        for filt in range(filts):
            for part, source in enumerate((cot_ref, sig_ref)):
                rows = source[pl.ds(owner * filts + filt, group, stride=count), :]
                out_ref[owner, pl.ds((part * filts + filt) * group, group), :] = rows
        out_ref[owner, pl.ds(2 * filts * group, filts), :] = fil_ref[pl.ds(owner * filts, filts), :]
        return carry

    lax.fori_loop(0, owners, one_owner, 0)


def unpack_kernel(plan, owners, in_ref, sig_ref, fil_ref):
    _, _, group, filts = plan
    count = owners * filts

    def one_owner(owner, carry):
        for filt in range(filts):
            sig_ref[pl.ds(owner * filts + filt, group, stride=count), :] = in_ref[owner, pl.ds(filt * group, group), :]
        fil_ref[pl.ds(owner * filts, filts), :] = in_ref[owner, pl.ds(filts * group, filts), :]
        return carry

    lax.fori_loop(0, owners, one_owner, 0)


def turn_blocks(value):
    rows = [value[at] for at in range(8)]
    sub = lax.broadcasted_iota(jnp.int32, rows[0].shape, 0)
    for bit in (1, 2, 4):
        clear = (sub & bit) == 0
        turned = list(rows)
        for at in range(8):
            if at & bit == 0:
                turned[at] = jnp.where(clear, rows[at], pltpu.roll(rows[at + bit], bit, 0))
                turned[at + bit] = jnp.where(clear, pltpu.roll(rows[at], 8 - bit, 0), rows[at + bit])
        rows = turned
    return rows


def pack_copied_kernel(plan, owners, chunks, cot_hbm, sig_hbm, fil_hbm, out_ref, cot_ref, sig_ref, sems, fil_sem):
    _, _, group, filts = plan
    many = owners // chunks
    span = many * filts
    copies = []
    for chunk in range(chunks):
        for part, (source, target) in enumerate(((cot_hbm, cot_ref), (sig_hbm, sig_ref))):
            rows = pl.ds(chunk * span, span)
            copies.append(pltpu.make_async_copy(source.at[:, rows, :], target.at[:, rows, :], sems.at[part, chunk]))
            copies[-1].start()
    fil_copy = pltpu.make_async_copy(fil_hbm, out_ref.at[:, pl.ds(2 * filts * group, filts), :], fil_sem)
    fil_copy.start()
    for chunk in range(chunks):
        for part, source in enumerate((cot_ref, sig_ref)):
            copies[2 * chunk + part].wait()
            for owner in range(chunk * many, (chunk + 1) * many):
                rows = turn_blocks(source[:, pl.ds(owner * filts, filts), :])
                for filt in range(filts):
                    out_ref[owner, pl.ds((part * filts + filt) * group, group), :] = rows[filt]
    fil_copy.wait()


def unpack_copied_kernel(plan, owners, chunks, in_ref, sig_hbm, fil_hbm, sig_ref, sems, fil_sem):
    _, _, group, filts = plan
    many = owners // chunks
    span = many * filts
    fil_copy = pltpu.make_async_copy(in_ref.at[:, pl.ds(filts * group, filts), :], fil_hbm, fil_sem)
    fil_copy.start()
    copies = []
    for chunk in range(chunks):
        for owner in range(chunk * many, (chunk + 1) * many):
            block = jnp.stack([in_ref[owner, pl.ds(filt * group, group), :] for filt in range(filts)], axis=0)
            for at, row in enumerate(turn_blocks(block)):
                sig_ref[at, pl.ds(owner * filts, filts), :] = row
        rows = pl.ds(chunk * span, span)
        copies.append(pltpu.make_async_copy(sig_ref.at[:, rows, :], sig_hbm.at[:, rows, :], sems.at[chunk]))
        copies[-1].start()
    for copy in copies:
        copy.wait()
    fil_copy.wait()


def pack_rows(plan, owners, cot, sig, fil):
    _, _, group, filts = plan
    channels, local = cot.shape
    out = jax.ShapeDtypeStruct((owners, 2 * filts * group + filts, local), f32)
    if (group, filts) != (8, 8):
        return vmem_call(functools.partial(pack_kernel, plan, owners), out, (cot, sig, fil), "pack_rows", 1e6)
    chunks = math.gcd(owners, 4)
    grouped = (group, channels // group, local)
    return pl.pallas_call(
        functools.partial(pack_copied_kernel, plan, owners, chunks),
        out_shape=out,
        in_specs=[pl.BlockSpec(memory_space=pl.ANY)] * 3,
        out_specs=pl.BlockSpec(memory_space=pltpu.VMEM),
        scratch_shapes=[pltpu.VMEM(grouped, f32)] * 2
        + [pltpu.SemaphoreType.DMA((2, chunks)), pltpu.SemaphoreType.DMA],
        compiler_params=pltpu.CompilerParams(vmem_limit_bytes=44 << 20),
        cost_estimate=pl.CostEstimate(flops=0, bytes_accessed=16 * cot.size, transcendentals=0),
        name="pack_rows",
    )(*[pltpu.with_memory_space_constraint(x, pltpu.HBM) for x in (cot.reshape(grouped), sig.reshape(grouped), fil.reshape(owners, filts, local))])


def unpack_rows(plan, owners, value):
    _, _, group, filts = plan
    count, local = owners * filts, value.shape[2]
    channels = group * count
    if (group, filts) != (8, 8):
        outs = [jax.ShapeDtypeStruct((channels, local), f32), jax.ShapeDtypeStruct((count, local), f32)]
        return vmem_call(functools.partial(unpack_kernel, plan, owners), outs, (value,), "unpack_rows", 1e6)
    chunks = math.gcd(owners, 4)
    grouped = (group, count, local)
    dsig, dfil = pl.pallas_call(
        functools.partial(unpack_copied_kernel, plan, owners, chunks),
        out_shape=[jax.ShapeDtypeStruct(grouped, f32), jax.ShapeDtypeStruct((owners, filts, local), f32)],
        in_specs=[pl.BlockSpec(memory_space=pltpu.VMEM)],
        out_specs=[pl.BlockSpec(memory_space=pl.ANY)] * 2,
        scratch_shapes=[pltpu.VMEM(grouped, f32), pltpu.SemaphoreType.DMA((chunks,)), pltpu.SemaphoreType.DMA],
        compiler_params=pltpu.CompilerParams(vmem_limit_bytes=44 << 20),
        cost_estimate=pl.CostEstimate(flops=0, bytes_accessed=8 * value.size, transcendentals=0),
        name="unpack_rows",
    )(value)
    return dsig.reshape(channels, local), dfil.reshape(count, local)


def body(signal, cotangent, filters):
    ranks, halves = lax.axis_size("ctx"), lax.axis_size("tp")
    channels, local = signal.shape
    count = filters.shape[0]
    both = count % (8 * ranks * halves) == 0
    axes, sources = (("ctx", "tp"), halves) if both else ("ctx", 1)
    owners = ranks * sources
    group, filts = channels // count, count // owners
    plan = (ranks, sources, group, filts)

    def exchange(value):
        return lax.all_to_all(value, axes, split_axis=0, concat_axis=0, tiled=True)

    data = exchange(pack_rows(plan, owners, cotangent, signal, filters))
    grad_signal, grad_filters = unpack_rows(plan, owners, exchange(call_gradients(plan, data)))
    if not both:
        grad_filters = lax.psum(grad_filters, "tp")
    return grad_signal, grad_filters


def solution(mesh):
    return jax.shard_map(
        body,
        mesh=mesh,
        in_specs=(P("tp", "ctx"), P("tp", "ctx"), P(None, "ctx")),
        out_specs=(P("tp", "ctx"), P(None, "ctx")),
        check_vma=False,
    )
```

```python
import functools
import math

import jax
import jax.numpy as jnp
from jax import lax
from jax.experimental import pallas as pl
from jax.experimental.pallas import tpu as pltpu
from jax.sharding import PartitionSpec as P

f32, bf16 = jnp.float32, jnp.bfloat16
PAIR = 256


def split_two(value):
    high = value.astype(bf16)
    low = (value - high.astype(f32)).astype(bf16)
    return high, low


def rotate_left(value, shift):
    half = value.shape[1] // 2
    if shift == half:
        return jnp.concatenate([value[:, half:], value[:, :half]], axis=1)
    return pltpu.roll(value, value.shape[1] - shift, 1)


def load_tile(ref, owner, start, group):
    if len(ref.shape) == 3:
        return ref[owner, pl.ds(start, group), :]
    high = ref.shape[2]
    return ref[owner, pl.ds(start // high, group // high), :, :].reshape(group, ref.shape[3])


def load_blocks(ref, start, blocks, sources, group):
    pieces = []
    for b in range(blocks):
        for s in range(sources):
            pieces.append(load_tile(ref, b * sources + s, start, group))
    even = jnp.concatenate([p for at, p in enumerate(pieces) if at // sources % 2 == 0], axis=0)
    odd = jnp.concatenate([p for at, p in enumerate(pieces) if at // sources % 2 == 1], axis=0)
    return jnp.concatenate([even, odd], axis=1)


def gradients_kernel(plan, data_ref, out_ref, lag_ref, *scratch):
    slots = [scratch[at : at + 6] for at in range(0, len(scratch), 6)]
    blocks, sources, group, filts = plan
    local = data_ref.shape[-1]
    pairs = blocks // 2
    step_rows = sources * group
    rows_all = pairs * step_rows
    length = blocks * local
    held = slots[0][2].dtype
    flip = lax.broadcasted_iota(jnp.int32, (local, local), 0) + lax.broadcasted_iota(jnp.int32, (local, local), 1)
    flip = jnp.where(flip == local - 1, 1.0, 0.0).astype(bf16)
    for *_, weight_ref, prod_ref in slots:
        weight_ref[pl.ds(3 * rows_all, 256), :] = jnp.zeros((256, PAIR), held)
        prod_ref[pairs] = jnp.zeros((PAIR, PAIR), f32)
    lane = lax.broadcasted_iota(jnp.int32, (8, PAIR), 1)
    sub = lax.broadcasted_iota(jnp.int32, (8 * pairs, PAIR), 0)
    ahead = lane[:, :128] - sub[:8, :128]

    for b in range(blocks):
        if len(data_ref.shape) == 3:
            lags = data_ref[b * sources, pl.ds(2 * filts * group, filts), :]
        else:
            parts = [data_ref[b * sources + s, 2 * filts * group // (filts // sources)] for s in range(sources)]
            lags = jnp.concatenate(parts, axis=0)
        high, low = split_two(lags)
        lag_ref[b] = jnp.dot(high, flip, preferred_element_type=f32) + jnp.dot(low, flip, preferred_element_type=f32)

    def one_filter(filt, slot):
        strip_high, strip_low, cot_high, cot_low, weight_ref, prod_ref = slots[slot]
        rows = load_blocks(data_ref, filt * group, blocks, sources, group)
        high, low = split_two(rows)
        cot_high[pl.ds(0, rows_all), :] = high.astype(held)
        cot_low[pl.ds(0, rows_all), :] = low.astype(held)
        for at in range(0, rows_all, step_rows):
            for turn_at, part in enumerate((high, low, high)):
                weight_ref[pl.ds(3 * at + turn_at * step_rows, step_rows), :] = part[at : at + step_rows].astype(held)

        back = [jnp.broadcast_to(lag_ref[b, pl.ds(filt, 1), :], (8, local)) for b in reversed(range(blocks))]
        back = jnp.concatenate(back + [jnp.zeros((8, PAIR), f32)], axis=1)
        skewed = pltpu.roll(back, 1, 1, stride=1, stride_axis=0)
        two = jnp.concatenate([skewed, pltpu.roll(skewed, 8, 1)], axis=0)
        high, low = split_two(two)
        high, low = high.astype(f32), low.astype(f32)
        for step in range(local // 16):
            strip_high[pl.ds(16 * step, 16), :] = pltpu.roll(high, 16 * step, 1).astype(bf16)
            strip_low[pl.ds(16 * step, 16), :] = pltpu.roll(low, 16 * step, 1).astype(bf16)

        sig = load_blocks(data_ref, (filts + filt) * group, blocks, sources, group)
        sig_high = sig.astype(bf16).astype(f32)
        sig_low = sig - sig_high
        stacked = []
        for at in range(0, rows_all, step_rows):
            stacked += [part[at : at + step_rows] for part in (sig_high, sig_high, sig_low)]
        turned = jnp.concatenate(stacked, axis=0).T.astype(bf16)
        for gap in range(pairs):
            deep = min(-(-3 * (rows_all - gap * step_rows) // 128) * 128, 3 * rows_all)
            weights = weight_ref[pl.ds(3 * gap * step_rows, deep), :].astype(bf16)
            prod_ref[gap] = jnp.dot(turned[:, :deep], weights, preferred_element_type=f32)

        total = None
        for gap in range(pairs):
            kept = rows_all - gap * step_rows
            high = cot_high[pl.ds(gap * step_rows, kept), :].astype(bf16)
            low = cot_low[pl.ds(gap * step_rows, kept), :].astype(bf16)
            at = length - gap * PAIR
            t_high = jnp.concatenate([strip_high[:, pl.ds(at, PAIR)], strip_high[:, pl.ds(at - local, PAIR)]], axis=0)
            t_low = jnp.concatenate([strip_low[:, pl.ds(at, PAIR)], strip_low[:, pl.ds(at - local, PAIR)]], axis=0)
            both = jnp.dot(jnp.concatenate([high, low], axis=0), t_high, preferred_element_type=f32)
            part = both[:kept] + both[kept:] + jnp.dot(high, t_low, preferred_element_type=f32)
            if total is None:
                total = part
            else:
                part = jnp.concatenate([part, jnp.zeros((gap * step_rows, PAIR), f32)], axis=0)
                total = total + part
        for b in range(blocks):
            for s in range(sources):
                at = b // 2 * step_rows + s * group
                piece = total[at : at + group, b % 2 * local : (b % 2 + 1) * local]
                out_ref[b * sources + s, pl.ds(filt * group, group), :] = piece

        def leaf(gap, step):
            near, far = pl.ds(8 * step, 8), pl.ds(8 * step + 128, 8)
            left, right = pl.ds(0, 128), pl.ds(128, 128)
            valid = ahead >= 8 * step
            first = jnp.where(valid, prod_ref[gap, near, left], prod_ref[gap + 1, near, left])
            second = jnp.where(valid, prod_ref[gap, far, right], prod_ref[gap + 1, far, right])
            return jnp.concatenate([first + second, prod_ref[gap, near, right] + prod_ref[gap + 1, far, left]], axis=1)

        lagged = []
        for gap in range(pairs):
            summed = leaf(gap, 0)
            for step in range(1, PAIR // 16):
                summed = summed + rotate_left(leaf(gap, step), 8 * step)
            lagged.append(summed)
        lagged = jnp.concatenate(lagged, axis=0)
        for bit in (1, 2, 4):
            lagged = jnp.where((sub & bit) != 0, rotate_left(lagged, bit), lagged)
        lagged = jnp.sum(lagged.reshape(pairs, 8, PAIR), axis=1)
        for gap in range(pairs):
            for s in range(sources):
                row = pl.ds(filts * group + filt, 1)
                out_ref[2 * gap * sources + s, row, :] = lagged[gap : gap + 1, :local]
                out_ref[(2 * gap + 1) * sources + s, row, :] = lagged[gap : gap + 1, local:]

    def some_filters(turn, carry):
        for slot in range(len(slots)):
            one_filter(turn * len(slots) + slot, slot)
        return carry

    lax.fori_loop(0, filts // len(slots), some_filters, 0)


def vmem_call(kernel, outs, args, name, flops, scratch=()):
    return pl.pallas_call(
        kernel,
        out_shape=outs,
        in_specs=[pl.BlockSpec(memory_space=pltpu.VMEM)] * len(args),
        out_specs=jax.tree.map(lambda _: pl.BlockSpec(memory_space=pltpu.VMEM), outs),
        scratch_shapes=list(scratch),
        compiler_params=pltpu.CompilerParams(vmem_limit_bytes=44 << 20),
        cost_estimate=pl.CostEstimate(
            flops=int(flops), bytes_accessed=sum(4 * a.size for a in args), transcendentals=0
        ),
        name=name,
    )(*args)


def call_gradients(plan, data):
    blocks, sources, group, filts = plan
    local = data.shape[-1]
    rows = blocks * sources * group
    held = bf16 if sources * group % 16 == 0 else f32
    scratch = (
        [pltpu.VMEM((local, blocks * local + PAIR), bf16)] * 2
        + [pltpu.VMEM((rows // 2, PAIR), held)] * 2
        + [pltpu.VMEM((3 * rows // 2 + 256, PAIR), held), pltpu.VMEM((blocks // 2 + 1, PAIR, PAIR), f32)]
    )
    scratch = [pltpu.VMEM((blocks, filts, local), f32)] + scratch * (2 if filts % 2 == 0 else 1)
    outs = jax.ShapeDtypeStruct((blocks * sources, filts * group + filts, local), f32)
    kernel = functools.partial(gradients_kernel, plan)
    return vmem_call(kernel, outs, (data,), "gradients", filts * 3e9, scratch)


def pack_kernel(plan, owners, cot_ref, sig_ref, fil_ref, out_ref):
    _, _, group, filts = plan
    count = owners * filts

    def one_owner(owner, carry):
        for filt in range(filts):
            for part, source in enumerate((cot_ref, sig_ref)):
                rows = source[pl.ds(owner * filts + filt, group, stride=count), :]
                out_ref[owner, pl.ds((part * filts + filt) * group, group), :] = rows
        out_ref[owner, pl.ds(2 * filts * group, filts), :] = fil_ref[pl.ds(owner * filts, filts), :]
        return carry

    lax.fori_loop(0, owners, one_owner, 0)


def unpack_kernel(plan, owners, in_ref, sig_ref, fil_ref):
    _, _, group, filts = plan
    count = owners * filts

    def one_owner(owner, carry):
        for filt in range(filts):
            sig_ref[pl.ds(owner * filts + filt, group, stride=count), :] = in_ref[owner, pl.ds(filt * group, group), :]
        fil_ref[pl.ds(owner * filts, filts), :] = in_ref[owner, pl.ds(filts * group, filts), :]
        return carry

    lax.fori_loop(0, owners, one_owner, 0)


def turn_blocks(value):
    rows = [value[at] for at in range(8)]
    sub = lax.broadcasted_iota(jnp.int32, rows[0].shape, 0)
    for bit in (1, 2, 4):
        clear = (sub & bit) == 0
        turned = list(rows)
        for at in range(8):
            if at & bit == 0:
                turned[at] = jnp.where(clear, rows[at], pltpu.roll(rows[at + bit], bit, 0))
                turned[at + bit] = jnp.where(clear, pltpu.roll(rows[at], 8 - bit, 0), rows[at + bit])
        rows = turned
    return rows


def pack_copied_kernel(plan, owners, chunks, cot_hbm, sig_hbm, fil_hbm, out_ref, cot_ref, sig_ref, fil_ref, sems, fil_sem):
    _, sources, group, filts = plan
    share = filts // sources
    many = owners // chunks
    span = many * filts
    copies = []
    for chunk in range(chunks):
        for part, (source, target) in enumerate(((cot_hbm, cot_ref), (sig_hbm, sig_ref))):
            rows = pl.ds(chunk * span, span)
            copies.append(pltpu.make_async_copy(source.at[:, rows, :], target.at[:, rows, :], sems.at[part, chunk]))
            copies[-1].start()
    fil_copy = pltpu.make_async_copy(fil_hbm, fil_ref, fil_sem)
    fil_copy.start()
    for chunk in range(chunks):
        for part, source in enumerate((cot_ref, sig_ref)):
            copies[2 * chunk + part].wait()
            for owner in range(chunk * many, (chunk + 1) * many):
                rows = turn_blocks(source[:, pl.ds(owner * filts, filts), :])
                for filt in range(filts):
                    at = (part * filts + filt) * group // share
                    out_ref[owner, pl.ds(at, group // share), :, :] = rows[filt].reshape(group // share, share, -1)
    fil_copy.wait()
    mine = lax.axis_index("tp")
    for owner in range(owners):
        kept = fil_ref[owner, pl.ds(0, share), :]
        for s in range(1, sources):
            kept = jnp.where(mine == s, fil_ref[owner, pl.ds(s * share, share), :], kept)
        out_ref[owner, 2 * filts * group // share] = kept


def unpack_copied_kernel(plan, owners, chunks, in_ref, sig_hbm, fil_hbm, sig_ref, sems, fil_sem):
    _, _, group, filts = plan
    many = owners // chunks
    span = many * filts
    fil_copy = pltpu.make_async_copy(in_ref.at[:, pl.ds(filts * group, filts), :], fil_hbm, fil_sem)
    fil_copy.start()
    copies = []
    for chunk in range(chunks):
        for owner in range(chunk * many, (chunk + 1) * many):
            block = jnp.stack([in_ref[owner, pl.ds(filt * group, group), :] for filt in range(filts)], axis=0)
            for at, row in enumerate(turn_blocks(block)):
                sig_ref[at, pl.ds(owner * filts, filts), :] = row
        rows = pl.ds(chunk * span, span)
        copies.append(pltpu.make_async_copy(sig_ref.at[:, rows, :], sig_hbm.at[:, rows, :], sems.at[chunk]))
        copies[-1].start()
    for copy in copies:
        copy.wait()
    fil_copy.wait()


def pack_rows(plan, owners, cot, sig, fil):
    _, sources, group, filts = plan
    channels, local = cot.shape
    out = jax.ShapeDtypeStruct((owners, 2 * filts * group + filts, local), f32)
    if (sources, group, filts) != (2, 8, 8):
        return vmem_call(functools.partial(pack_kernel, plan, owners), out, (cot, sig, fil), "pack_rows", 1e6)
    share = filts // sources
    out = jax.ShapeDtypeStruct((owners, 2 * filts * group // share + 1, share, local), f32)
    chunks = math.gcd(owners, 4)
    grouped = (group, channels // group, local)
    return pl.pallas_call(
        functools.partial(pack_copied_kernel, plan, owners, chunks),
        out_shape=out,
        in_specs=[pl.BlockSpec(memory_space=pl.ANY)] * 3,
        out_specs=pl.BlockSpec(memory_space=pltpu.VMEM),
        scratch_shapes=[pltpu.VMEM(grouped, f32)] * 2
        + [pltpu.VMEM((owners, filts, local), f32)]
        + [pltpu.SemaphoreType.DMA((2, chunks)), pltpu.SemaphoreType.DMA],
        compiler_params=pltpu.CompilerParams(vmem_limit_bytes=44 << 20),
        cost_estimate=pl.CostEstimate(flops=0, bytes_accessed=16 * cot.size, transcendentals=0),
        name="pack_rows",
    )(*[pltpu.with_memory_space_constraint(x, pltpu.HBM) for x in (cot.reshape(grouped), sig.reshape(grouped), fil.reshape(owners, filts, local))])


def unpack_rows(plan, owners, value):
    _, _, group, filts = plan
    count, local = owners * filts, value.shape[2]
    channels = group * count
    if (group, filts) != (8, 8):
        outs = [jax.ShapeDtypeStruct((channels, local), f32), jax.ShapeDtypeStruct((count, local), f32)]
        return vmem_call(functools.partial(unpack_kernel, plan, owners), outs, (value,), "unpack_rows", 1e6)
    chunks = math.gcd(owners, 4)
    grouped = (group, count, local)
    dsig, dfil = pl.pallas_call(
        functools.partial(unpack_copied_kernel, plan, owners, chunks),
        out_shape=[jax.ShapeDtypeStruct(grouped, f32), jax.ShapeDtypeStruct((owners, filts, local), f32)],
        in_specs=[pl.BlockSpec(memory_space=pltpu.VMEM)],
        out_specs=[pl.BlockSpec(memory_space=pl.ANY)] * 2,
        scratch_shapes=[pltpu.VMEM(grouped, f32), pltpu.SemaphoreType.DMA((chunks,)), pltpu.SemaphoreType.DMA],
        compiler_params=pltpu.CompilerParams(vmem_limit_bytes=44 << 20),
        cost_estimate=pl.CostEstimate(flops=0, bytes_accessed=8 * value.size, transcendentals=0),
        name="unpack_rows",
    )(value)
    return dsig.reshape(channels, local), dfil.reshape(count, local)


def body(signal, cotangent, filters):
    ranks, halves = lax.axis_size("ctx"), lax.axis_size("tp")
    channels, local = signal.shape
    count = filters.shape[0]
    both = count % (8 * ranks * halves) == 0
    axes, sources = (("ctx", "tp"), halves) if both else ("ctx", 1)
    owners = ranks * sources
    group, filts = channels // count, count // owners
    plan = (ranks, sources, group, filts)

    def exchange(value):
        return lax.all_to_all(value, axes, split_axis=0, concat_axis=0, tiled=True)

    data = exchange(pack_rows(plan, owners, cotangent, signal, filters))
    grad_signal, grad_filters = unpack_rows(plan, owners, exchange(call_gradients(plan, data)))
    if not both:
        grad_filters = lax.psum(grad_filters, "tp")
    return grad_signal, grad_filters


def solution(mesh):
    return jax.shard_map(
        body,
        mesh=mesh,
        in_specs=(P("tp", "ctx"), P("tp", "ctx"), P(None, "ctx")),
        out_specs=(P("tp", "ctx"), P(None, "ctx")),
        check_vma=False,
    )
```

```python
import functools
import math

import jax
import jax.numpy as jnp
from jax import lax
from jax.experimental import pallas as pl
from jax.experimental.pallas import tpu as pltpu
from jax.sharding import PartitionSpec as P

f32, bf16 = jnp.float32, jnp.bfloat16
PAIR = 256


def split_two(value):
    high = value.astype(bf16)
    low = (value - high.astype(f32)).astype(bf16)
    return high, low


def rotate_left(value, shift):
    half = value.shape[1] // 2
    if shift == half:
        return jnp.concatenate([value[:, half:], value[:, :half]], axis=1)
    return pltpu.roll(value, value.shape[1] - shift, 1)


def load_tile(ref, owner, start, group):
    if len(ref.shape) == 3:
        return ref[owner, pl.ds(start, group), :]
    high = ref.shape[2]
    return ref[owner, pl.ds(start // high, group // high), :, :].reshape(group, ref.shape[3])


def load_blocks(ref, start, blocks, sources, group):
    pieces = []
    for b in range(blocks):
        for s in range(sources):
            pieces.append(load_tile(ref, b * sources + s, start, group))
    even = jnp.concatenate([p for at, p in enumerate(pieces) if at // sources % 2 == 0], axis=0)
    odd = jnp.concatenate([p for at, p in enumerate(pieces) if at // sources % 2 == 1], axis=0)
    return jnp.concatenate([even, odd], axis=1)


def gradients_kernel(plan, data_ref, out_ref, lag_ref, *scratch):
    slots = [scratch[at : at + 6] for at in range(0, len(scratch), 6)]
    blocks, sources, group, filts = plan
    local = data_ref.shape[-1]
    pairs = blocks // 2
    step_rows = sources * group
    rows_all = pairs * step_rows
    length = blocks * local
    held = slots[0][2].dtype
    flip = lax.broadcasted_iota(jnp.int32, (local, local), 0) + lax.broadcasted_iota(jnp.int32, (local, local), 1)
    flip = jnp.where(flip == local - 1, 1.0, 0.0).astype(bf16)
    for *_, weight_ref, prod_ref in slots:
        weight_ref[pl.ds(3 * rows_all, 256), :] = jnp.zeros((256, PAIR), held)
        prod_ref[pairs] = jnp.zeros((PAIR, PAIR), f32)
    lane = lax.broadcasted_iota(jnp.int32, (8, PAIR), 1)
    sub = lax.broadcasted_iota(jnp.int32, (8 * pairs, PAIR), 0)
    ahead = lane[:, :128] - sub[:8, :128]

    for b in range(blocks):
        if len(data_ref.shape) == 3:
            lags = data_ref[b * sources, pl.ds(2 * filts * group, filts), :]
        else:
            parts = [data_ref[b * sources + s, 2 * filts * group // (filts // sources)] for s in range(sources)]
            lags = jnp.concatenate(parts, axis=0)
        high, low = split_two(lags)
        lag_ref[b] = jnp.dot(high, flip, preferred_element_type=f32) + jnp.dot(low, flip, preferred_element_type=f32)

    def one_filter(filt, slot):
        strip_high, strip_low, cot_high, cot_low, weight_ref, prod_ref = slots[slot]
        rows = load_blocks(data_ref, filt * group, blocks, sources, group)
        high, low = split_two(rows)
        cot_high[pl.ds(0, rows_all), :] = high.astype(held)
        cot_low[pl.ds(0, rows_all), :] = low.astype(held)
        for at in range(0, rows_all, step_rows):
            for turn_at, part in enumerate((high, low, high)):
                weight_ref[pl.ds(3 * at + turn_at * step_rows, step_rows), :] = part[at : at + step_rows].astype(held)

        back = [jnp.broadcast_to(lag_ref[b, pl.ds(filt, 1), :], (8, local)) for b in reversed(range(blocks))]
        back = jnp.concatenate(back + [jnp.zeros((8, PAIR), f32)], axis=1)
        skewed = pltpu.roll(back, 1, 1, stride=1, stride_axis=0)
        two = jnp.concatenate([skewed, pltpu.roll(skewed, 8, 1)], axis=0)
        high, low = split_two(two)
        high, low = high.astype(f32), low.astype(f32)
        for step in range(local // 16):
            strip_high[pl.ds(16 * step, 16), :] = pltpu.roll(high, 16 * step, 1).astype(bf16)
            strip_low[pl.ds(16 * step, 16), :] = pltpu.roll(low, 16 * step, 1).astype(bf16)

        sig = load_blocks(data_ref, (filts + filt) * group, blocks, sources, group)
        sig_high = sig.astype(bf16).astype(f32)
        sig_low = sig - sig_high
        stacked = []
        for at in range(0, rows_all, step_rows):
            stacked += [part[at : at + step_rows] for part in (sig_high, sig_high, sig_low)]
        turned = jnp.concatenate(stacked, axis=0).T.astype(bf16)
        for gap in range(pairs):
            deep = min(-(-3 * (rows_all - gap * step_rows) // 128) * 128, 3 * rows_all)
            weights = weight_ref[pl.ds(3 * gap * step_rows, deep), :].astype(bf16)
            prod_ref[gap] = jnp.dot(turned[:, :deep], weights, preferred_element_type=f32)
            yield

        total = None
        for gap in range(pairs):
            kept = rows_all - gap * step_rows
            high = cot_high[pl.ds(gap * step_rows, kept), :].astype(bf16)
            low = cot_low[pl.ds(gap * step_rows, kept), :].astype(bf16)
            at = length - gap * PAIR
            t_high = jnp.concatenate([strip_high[:, pl.ds(at, PAIR)], strip_high[:, pl.ds(at - local, PAIR)]], axis=0)
            t_low = jnp.concatenate([strip_low[:, pl.ds(at, PAIR)], strip_low[:, pl.ds(at - local, PAIR)]], axis=0)
            both = jnp.dot(jnp.concatenate([high, low], axis=0), t_high, preferred_element_type=f32)
            part = both[:kept] + both[kept:] + jnp.dot(high, t_low, preferred_element_type=f32)
            if total is None:
                total = part
            else:
                part = jnp.concatenate([part, jnp.zeros((gap * step_rows, PAIR), f32)], axis=0)
                total = total + part
        for b in range(blocks):
            for s in range(sources):
                at = b // 2 * step_rows + s * group
                piece = total[at : at + group, b % 2 * local : (b % 2 + 1) * local]
                out_ref[b * sources + s, pl.ds(filt * group, group), :] = piece

        def leaf(gap, step):
            near, far = pl.ds(8 * step, 8), pl.ds(8 * step + 128, 8)
            left, right = pl.ds(0, 128), pl.ds(128, 128)
            valid = ahead >= 8 * step
            first = jnp.where(valid, prod_ref[gap, near, left], prod_ref[gap + 1, near, left])
            second = jnp.where(valid, prod_ref[gap, far, right], prod_ref[gap + 1, far, right])
            return jnp.concatenate([first + second, prod_ref[gap, near, right] + prod_ref[gap + 1, far, left]], axis=1)

        lagged = []
        for gap in range(pairs):
            summed = leaf(gap, 0)
            for step in range(1, PAIR // 16):
                summed = summed + rotate_left(leaf(gap, step), 8 * step)
            lagged.append(summed)
        lagged = jnp.concatenate(lagged, axis=0)
        for bit in (1, 2, 4):
            lagged = jnp.where((sub & bit) != 0, rotate_left(lagged, bit), lagged)
        lagged = jnp.sum(lagged.reshape(pairs, 8, PAIR), axis=1)
        for gap in range(pairs):
            for s in range(sources):
                row = pl.ds(filts * group + filt, 1)
                out_ref[2 * gap * sources + s, row, :] = lagged[gap : gap + 1, :local]
                out_ref[(2 * gap + 1) * sources + s, row, :] = lagged[gap : gap + 1, local:]

    def some_filters(turn, carry):
        stages = [one_filter(turn * len(slots) + slot, slot) for slot in range(len(slots))]
        while stages:
            stages = [stage for stage in stages if next(stage, 1) is None]
        return carry

    lax.fori_loop(0, filts // len(slots), some_filters, 0)


def vmem_call(kernel, outs, args, name, flops, scratch=()):
    return pl.pallas_call(
        kernel,
        out_shape=outs,
        in_specs=[pl.BlockSpec(memory_space=pltpu.VMEM)] * len(args),
        out_specs=jax.tree.map(lambda _: pl.BlockSpec(memory_space=pltpu.VMEM), outs),
        scratch_shapes=list(scratch),
        compiler_params=pltpu.CompilerParams(vmem_limit_bytes=44 << 20),
        cost_estimate=pl.CostEstimate(
            flops=int(flops), bytes_accessed=sum(4 * a.size for a in args), transcendentals=0
        ),
        name=name,
    )(*args)


def call_gradients(plan, data):
    blocks, sources, group, filts = plan
    local = data.shape[-1]
    rows = blocks * sources * group
    held = bf16 if sources * group % 16 == 0 else f32
    scratch = (
        [pltpu.VMEM((local, blocks * local + PAIR), bf16)] * 2
        + [pltpu.VMEM((rows // 2, PAIR), held)] * 2
        + [pltpu.VMEM((3 * rows // 2 + 256, PAIR), held), pltpu.VMEM((blocks // 2 + 1, PAIR, PAIR), f32)]
    )
    scratch = [pltpu.VMEM((blocks, filts, local), f32)] + scratch * (2 if filts % 2 == 0 else 1)
    outs = jax.ShapeDtypeStruct((blocks * sources, filts * group + filts, local), f32)
    kernel = functools.partial(gradients_kernel, plan)
    return vmem_call(kernel, outs, (data,), "gradients", filts * 3e9, scratch)


def pack_kernel(plan, owners, cot_ref, sig_ref, fil_ref, out_ref):
    _, _, group, filts = plan
    count = owners * filts

    def one_owner(owner, carry):
        for filt in range(filts):
            for part, source in enumerate((cot_ref, sig_ref)):
                rows = source[pl.ds(owner * filts + filt, group, stride=count), :]
                out_ref[owner, pl.ds((part * filts + filt) * group, group), :] = rows
        out_ref[owner, pl.ds(2 * filts * group, filts), :] = fil_ref[pl.ds(owner * filts, filts), :]
        return carry

    lax.fori_loop(0, owners, one_owner, 0)


def unpack_kernel(plan, owners, in_ref, sig_ref, fil_ref):
    _, _, group, filts = plan
    count = owners * filts

    def one_owner(owner, carry):
        for filt in range(filts):
            sig_ref[pl.ds(owner * filts + filt, group, stride=count), :] = in_ref[owner, pl.ds(filt * group, group), :]
        fil_ref[pl.ds(owner * filts, filts), :] = in_ref[owner, pl.ds(filts * group, filts), :]
        return carry

    lax.fori_loop(0, owners, one_owner, 0)


def turn_blocks(value):
    rows = [value[at] for at in range(8)]
    sub = lax.broadcasted_iota(jnp.int32, rows[0].shape, 0)
    for bit in (1, 2, 4):
        clear = (sub & bit) == 0
        turned = list(rows)
        for at in range(8):
            if at & bit == 0:
                turned[at] = jnp.where(clear, rows[at], pltpu.roll(rows[at + bit], bit, 0))
                turned[at + bit] = jnp.where(clear, pltpu.roll(rows[at], 8 - bit, 0), rows[at + bit])
        rows = turned
    return rows


def pack_copied_kernel(plan, owners, chunks, cot_hbm, sig_hbm, fil_hbm, out_ref, cot_ref, sig_ref, fil_ref, sems, fil_sem):
    _, sources, group, filts = plan
    share = filts // sources
    many = owners // chunks
    span = many * filts
    copies = []
    for chunk in range(chunks):
        for part, (source, target) in enumerate(((cot_hbm, cot_ref), (sig_hbm, sig_ref))):
            rows = pl.ds(chunk * span, span)
            copies.append(pltpu.make_async_copy(source.at[:, rows, :], target.at[:, rows, :], sems.at[part, chunk]))
            copies[-1].start()
    fil_copy = pltpu.make_async_copy(fil_hbm, fil_ref, fil_sem)
    fil_copy.start()
    for chunk in range(chunks):
        for part, source in enumerate((cot_ref, sig_ref)):
            copies[2 * chunk + part].wait()
            for owner in range(chunk * many, (chunk + 1) * many):
                rows = turn_blocks(source[:, pl.ds(owner * filts, filts), :])
                for filt in range(filts):
                    at = (part * filts + filt) * group // share
                    out_ref[owner, pl.ds(at, group // share), :, :] = rows[filt].reshape(group // share, share, -1)
    fil_copy.wait()
    mine = lax.axis_index("tp")
    for owner in range(owners):
        kept = fil_ref[owner, pl.ds(0, share), :]
        for s in range(1, sources):
            kept = jnp.where(mine == s, fil_ref[owner, pl.ds(s * share, share), :], kept)
        out_ref[owner, 2 * filts * group // share] = kept


def unpack_copied_kernel(plan, owners, chunks, in_ref, sig_hbm, fil_hbm, sig_ref, sems, fil_sem):
    _, _, group, filts = plan
    many = owners // chunks
    span = many * filts
    fil_copy = pltpu.make_async_copy(in_ref.at[:, pl.ds(filts * group, filts), :], fil_hbm, fil_sem)
    fil_copy.start()
    copies = []
    for chunk in range(chunks):
        for owner in range(chunk * many, (chunk + 1) * many):
            block = jnp.stack([in_ref[owner, pl.ds(filt * group, group), :] for filt in range(filts)], axis=0)
            for at, row in enumerate(turn_blocks(block)):
                sig_ref[at, pl.ds(owner * filts, filts), :] = row
        rows = pl.ds(chunk * span, span)
        copies.append(pltpu.make_async_copy(sig_ref.at[:, rows, :], sig_hbm.at[:, rows, :], sems.at[chunk]))
        copies[-1].start()
    for copy in copies:
        copy.wait()
    fil_copy.wait()


def pack_rows(plan, owners, cot, sig, fil):
    _, sources, group, filts = plan
    channels, local = cot.shape
    out = jax.ShapeDtypeStruct((owners, 2 * filts * group + filts, local), f32)
    if (sources, group, filts) != (2, 8, 8):
        return vmem_call(functools.partial(pack_kernel, plan, owners), out, (cot, sig, fil), "pack_rows", 1e6)
    share = filts // sources
    out = jax.ShapeDtypeStruct((owners, 2 * filts * group // share + 1, share, local), f32)
    chunks = math.gcd(owners, 4)
    grouped = (group, channels // group, local)
    return pl.pallas_call(
        functools.partial(pack_copied_kernel, plan, owners, chunks),
        out_shape=out,
        in_specs=[pl.BlockSpec(memory_space=pl.ANY)] * 3,
        out_specs=pl.BlockSpec(memory_space=pltpu.VMEM),
        scratch_shapes=[pltpu.VMEM(grouped, f32)] * 2
        + [pltpu.VMEM((owners, filts, local), f32)]
        + [pltpu.SemaphoreType.DMA((2, chunks)), pltpu.SemaphoreType.DMA],
        compiler_params=pltpu.CompilerParams(vmem_limit_bytes=44 << 20),
        cost_estimate=pl.CostEstimate(flops=0, bytes_accessed=16 * cot.size, transcendentals=0),
        name="pack_rows",
    )(*[pltpu.with_memory_space_constraint(x, pltpu.HBM) for x in (cot.reshape(grouped), sig.reshape(grouped), fil.reshape(owners, filts, local))])


def unpack_rows(plan, owners, value):
    _, _, group, filts = plan
    count, local = owners * filts, value.shape[2]
    channels = group * count
    if (group, filts) != (8, 8):
        outs = [jax.ShapeDtypeStruct((channels, local), f32), jax.ShapeDtypeStruct((count, local), f32)]
        return vmem_call(functools.partial(unpack_kernel, plan, owners), outs, (value,), "unpack_rows", 1e6)
    chunks = math.gcd(owners, 4)
    grouped = (group, count, local)
    dsig, dfil = pl.pallas_call(
        functools.partial(unpack_copied_kernel, plan, owners, chunks),
        out_shape=[jax.ShapeDtypeStruct(grouped, f32), jax.ShapeDtypeStruct((owners, filts, local), f32)],
        in_specs=[pl.BlockSpec(memory_space=pltpu.VMEM)],
        out_specs=[pl.BlockSpec(memory_space=pl.ANY)] * 2,
        scratch_shapes=[pltpu.VMEM(grouped, f32), pltpu.SemaphoreType.DMA((chunks,)), pltpu.SemaphoreType.DMA],
        compiler_params=pltpu.CompilerParams(vmem_limit_bytes=44 << 20),
        cost_estimate=pl.CostEstimate(flops=0, bytes_accessed=8 * value.size, transcendentals=0),
        name="unpack_rows",
    )(value)
    return dsig.reshape(channels, local), dfil.reshape(count, local)


def body(signal, cotangent, filters):
    ranks, halves = lax.axis_size("ctx"), lax.axis_size("tp")
    channels, local = signal.shape
    count = filters.shape[0]
    both = count % (8 * ranks * halves) == 0
    axes, sources = (("ctx", "tp"), halves) if both else ("ctx", 1)
    owners = ranks * sources
    group, filts = channels // count, count // owners
    plan = (ranks, sources, group, filts)

    def exchange(value):
        return lax.all_to_all(value, axes, split_axis=0, concat_axis=0, tiled=True)

    data = exchange(pack_rows(plan, owners, cotangent, signal, filters))
    grad_signal, grad_filters = unpack_rows(plan, owners, exchange(call_gradients(plan, data)))
    if not both:
        grad_filters = lax.psum(grad_filters, "tp")
    return grad_signal, grad_filters


def solution(mesh):
    return jax.shard_map(
        body,
        mesh=mesh,
        in_specs=(P("tp", "ctx"), P("tp", "ctx"), P(None, "ctx")),
        out_specs=(P("tp", "ctx"), P(None, "ctx")),
        check_vma=False,
    )
```

```python
import functools
import math

import jax
import jax.numpy as jnp
from jax import lax
from jax.experimental import pallas as pl
from jax.experimental.pallas import tpu as pltpu
from jax.sharding import PartitionSpec as P

f32, bf16 = jnp.float32, jnp.bfloat16
PAIR = 256


def split_two(value):
    high = value.astype(bf16)
    low = (value - high.astype(f32)).astype(bf16)
    return high, low


def rotate_left(value, shift):
    half = value.shape[1] // 2
    if shift == half:
        return jnp.concatenate([value[:, half:], value[:, :half]], axis=1)
    return pltpu.roll(value, value.shape[1] - shift, 1)


def load_tile(ref, owner, start, group):
    if len(ref.shape) == 3:
        return ref[owner, pl.ds(start, group), :]
    high = ref.shape[2]
    return ref[owner, pl.ds(start // high, group // high), :, :].reshape(group, ref.shape[3])


def load_blocks(ref, start, blocks, sources, group):
    pieces = []
    for b in range(blocks):
        for s in range(sources):
            pieces.append(load_tile(ref, b * sources + s, start, group))
    even = jnp.concatenate([p for at, p in enumerate(pieces) if at // sources % 2 == 0], axis=0)
    odd = jnp.concatenate([p for at, p in enumerate(pieces) if at // sources % 2 == 1], axis=0)
    return jnp.concatenate([even, odd], axis=1)


def gradients_kernel(plan, data_ref, out_ref, lag_ref, *scratch):
    slots = [scratch[at : at + 6] for at in range(0, len(scratch), 6)]
    blocks, sources, group, filts = plan
    local = data_ref.shape[-1]
    pairs = blocks // 2
    step_rows = sources * group
    rows_all = pairs * step_rows
    length = blocks * local
    held = slots[0][2].dtype
    flip = lax.broadcasted_iota(jnp.int32, (local, local), 0) + lax.broadcasted_iota(jnp.int32, (local, local), 1)
    flip = jnp.where(flip == local - 1, 1.0, 0.0).astype(bf16)
    for *_, weight_ref, prod_ref in slots:
        weight_ref[pl.ds(3 * rows_all, 256), :] = jnp.zeros((256, PAIR), held)
        prod_ref[pairs] = jnp.zeros((PAIR, PAIR), f32)
    lane = lax.broadcasted_iota(jnp.int32, (8, PAIR), 1)
    sub = lax.broadcasted_iota(jnp.int32, (8 * pairs, PAIR), 0)
    ahead = lane[:, :128] - sub[:8, :128]

    for b in range(blocks):
        if len(data_ref.shape) == 3:
            lags = data_ref[b * sources, pl.ds(2 * filts * group, filts), :]
        else:
            parts = [data_ref[b * sources + s, 2 * filts * group // (filts // sources)] for s in range(sources)]
            lags = jnp.concatenate(parts, axis=0)
        high, low = split_two(lags)
        lag_ref[b] = jnp.dot(high, flip, preferred_element_type=f32) + jnp.dot(low, flip, preferred_element_type=f32)

    def one_filter(filt, slot):
        strip_high, strip_low, cot_high, cot_low, weight_ref, prod_ref = slots[slot]
        rows = load_blocks(data_ref, filt * group, blocks, sources, group)
        high, low = split_two(rows)
        cot_high[pl.ds(0, rows_all), :] = high.astype(held)
        cot_low[pl.ds(0, rows_all), :] = low.astype(held)
        for at in range(0, rows_all, step_rows):
            for turn_at, part in enumerate((high, low, high)):
                weight_ref[pl.ds(3 * at + turn_at * step_rows, step_rows), :] = part[at : at + step_rows].astype(held)

        back = [jnp.broadcast_to(lag_ref[b, pl.ds(filt, 1), :], (8, local)) for b in reversed(range(blocks))]
        back = jnp.concatenate(back + [jnp.zeros((8, PAIR), f32)], axis=1)
        skewed = pltpu.roll(back, 1, 1, stride=1, stride_axis=0)
        two = jnp.concatenate([skewed, pltpu.roll(skewed, 8, 1)], axis=0)
        high, low = split_two(two)
        high, low = high.astype(f32), low.astype(f32)
        for step in range(local // 16):
            strip_high[pl.ds(16 * step, 16), :] = pltpu.roll(high, 16 * step, 1).astype(bf16)
            strip_low[pl.ds(16 * step, 16), :] = pltpu.roll(low, 16 * step, 1).astype(bf16)

        sig = load_blocks(data_ref, (filts + filt) * group, blocks, sources, group)
        sig_high = sig.astype(bf16).astype(f32)
        sig_low = sig - sig_high
        stacked = []
        for at in range(0, rows_all, step_rows):
            stacked += [part[at : at + step_rows] for part in (sig_high, sig_high, sig_low)]
        turned = jnp.concatenate(stacked, axis=0).T.astype(bf16)
        for gap in range(pairs):
            deep = min(-(-3 * (rows_all - gap * step_rows) // 128) * 128, 3 * rows_all)
            weights = weight_ref[pl.ds(3 * gap * step_rows, deep), :].astype(bf16)
            prod_ref[gap] = jnp.dot(turned[:, :deep], weights, preferred_element_type=f32)
            yield

        total = None
        for gap in range(pairs):
            kept = rows_all - gap * step_rows
            high = cot_high[pl.ds(gap * step_rows, kept), :].astype(bf16)
            low = cot_low[pl.ds(gap * step_rows, kept), :].astype(bf16)
            at = length - gap * PAIR
            t_high = jnp.concatenate([strip_high[:, pl.ds(at, PAIR)], strip_high[:, pl.ds(at - local, PAIR)]], axis=0)
            t_low = jnp.concatenate([strip_low[:, pl.ds(at, PAIR)], strip_low[:, pl.ds(at - local, PAIR)]], axis=0)
            both = jnp.dot(jnp.concatenate([high, low], axis=0), t_high, preferred_element_type=f32)
            part = both[:kept] + both[kept:] + jnp.dot(high, t_low, preferred_element_type=f32)
            if total is None:
                total = part
            else:
                part = jnp.concatenate([part, jnp.zeros((gap * step_rows, PAIR), f32)], axis=0)
                total = total + part
        for b in range(blocks):
            for s in range(sources):
                at = b // 2 * step_rows + s * group
                piece = total[at : at + group, b % 2 * local : (b % 2 + 1) * local]
                out_ref[b * sources + s, pl.ds(filt * group, group), :] = piece

        def leaf(gap, step):
            near, far = pl.ds(8 * step, 8), pl.ds(8 * step + 128, 8)
            left, right = pl.ds(0, 128), pl.ds(128, 128)
            valid = ahead >= 8 * step
            first = jnp.where(valid, prod_ref[gap, near, left], prod_ref[gap + 1, near, left])
            second = jnp.where(valid, prod_ref[gap, far, right], prod_ref[gap + 1, far, right])
            return jnp.concatenate([first + second, prod_ref[gap, near, right] + prod_ref[gap + 1, far, left]], axis=1)

        lagged = []
        for gap in range(pairs):
            summed = leaf(gap, 0)
            for step in range(1, PAIR // 16):
                summed = summed + rotate_left(leaf(gap, step), 8 * step)
            lagged.append(summed)
            yield
        lagged = jnp.concatenate(lagged, axis=0)
        for bit in (1, 2, 4):
            lagged = jnp.where((sub & bit) != 0, rotate_left(lagged, bit), lagged)
        lagged = jnp.sum(lagged.reshape(pairs, 8, PAIR), axis=1)
        for gap in range(pairs):
            for s in range(sources):
                row = pl.ds(filts * group + filt, 1)
                out_ref[2 * gap * sources + s, row, :] = lagged[gap : gap + 1, :local]
                out_ref[(2 * gap + 1) * sources + s, row, :] = lagged[gap : gap + 1, local:]

    def some_filters(turn, carry):
        stages = [one_filter(turn * len(slots) + slot, slot) for slot in range(len(slots))]
        while stages:
            stages = [stage for stage in stages if next(stage, 1) is None]
        return carry

    lax.fori_loop(0, filts // len(slots), some_filters, 0)


def vmem_call(kernel, outs, args, name, flops, scratch=()):
    return pl.pallas_call(
        kernel,
        out_shape=outs,
        in_specs=[pl.BlockSpec(memory_space=pltpu.VMEM)] * len(args),
        out_specs=jax.tree.map(lambda _: pl.BlockSpec(memory_space=pltpu.VMEM), outs),
        scratch_shapes=list(scratch),
        compiler_params=pltpu.CompilerParams(vmem_limit_bytes=44 << 20),
        cost_estimate=pl.CostEstimate(
            flops=int(flops), bytes_accessed=sum(4 * a.size for a in args), transcendentals=0
        ),
        name=name,
    )(*args)


def call_gradients(plan, data):
    blocks, sources, group, filts = plan
    local = data.shape[-1]
    rows = blocks * sources * group
    held = bf16 if sources * group % 16 == 0 else f32
    scratch = (
        [pltpu.VMEM((local, blocks * local + PAIR), bf16)] * 2
        + [pltpu.VMEM((rows // 2, PAIR), held)] * 2
        + [pltpu.VMEM((3 * rows // 2 + 256, PAIR), held), pltpu.VMEM((blocks // 2 + 1, PAIR, PAIR), f32)]
    )
    scratch = [pltpu.VMEM((blocks, filts, local), f32)] + scratch * (2 if filts % 2 == 0 else 1)
    outs = jax.ShapeDtypeStruct((blocks * sources, filts * group + filts, local), f32)
    kernel = functools.partial(gradients_kernel, plan)
    return vmem_call(kernel, outs, (data,), "gradients", filts * 3e9, scratch)


def pack_kernel(plan, owners, cot_ref, sig_ref, fil_ref, out_ref):
    _, _, group, filts = plan
    count = owners * filts

    def one_owner(owner, carry):
        for filt in range(filts):
            for part, source in enumerate((cot_ref, sig_ref)):
                rows = source[pl.ds(owner * filts + filt, group, stride=count), :]
                out_ref[owner, pl.ds((part * filts + filt) * group, group), :] = rows
        out_ref[owner, pl.ds(2 * filts * group, filts), :] = fil_ref[pl.ds(owner * filts, filts), :]
        return carry

    lax.fori_loop(0, owners, one_owner, 0)


def unpack_kernel(plan, owners, in_ref, sig_ref, fil_ref):
    _, _, group, filts = plan
    count = owners * filts

    def one_owner(owner, carry):
        for filt in range(filts):
            sig_ref[pl.ds(owner * filts + filt, group, stride=count), :] = in_ref[owner, pl.ds(filt * group, group), :]
        fil_ref[pl.ds(owner * filts, filts), :] = in_ref[owner, pl.ds(filts * group, filts), :]
        return carry

    lax.fori_loop(0, owners, one_owner, 0)


def turn_blocks(value):
    rows = [value[at] for at in range(8)]
    sub = lax.broadcasted_iota(jnp.int32, rows[0].shape, 0)
    for bit in (1, 2, 4):
        clear = (sub & bit) == 0
        turned = list(rows)
        for at in range(8):
            if at & bit == 0:
                turned[at] = jnp.where(clear, rows[at], pltpu.roll(rows[at + bit], bit, 0))
                turned[at + bit] = jnp.where(clear, pltpu.roll(rows[at], 8 - bit, 0), rows[at + bit])
        rows = turned
    return rows


def pack_copied_kernel(plan, owners, chunks, cot_hbm, sig_hbm, fil_hbm, out_ref, cot_ref, sig_ref, fil_ref, sems, fil_sem):
    _, sources, group, filts = plan
    share = filts // sources
    many = owners // chunks
    span = many * filts
    copies = []
    for chunk in range(chunks):
        for part, (source, target) in enumerate(((cot_hbm, cot_ref), (sig_hbm, sig_ref))):
            rows = pl.ds(chunk * span, span)
            copies.append(pltpu.make_async_copy(source.at[:, rows, :], target.at[:, rows, :], sems.at[part, chunk]))
            copies[-1].start()
    fil_copy = pltpu.make_async_copy(fil_hbm, fil_ref, fil_sem)
    fil_copy.start()
    for chunk in range(chunks):
        for part, source in enumerate((cot_ref, sig_ref)):
            copies[2 * chunk + part].wait()
            for owner in range(chunk * many, (chunk + 1) * many):
                rows = turn_blocks(source[:, pl.ds(owner * filts, filts), :])
                for filt in range(filts):
                    at = (part * filts + filt) * group // share
                    out_ref[owner, pl.ds(at, group // share), :, :] = rows[filt].reshape(group // share, share, -1)
    fil_copy.wait()
    mine = lax.axis_index("tp")
    for owner in range(owners):
        kept = fil_ref[owner, pl.ds(0, share), :]
        for s in range(1, sources):
            kept = jnp.where(mine == s, fil_ref[owner, pl.ds(s * share, share), :], kept)
        out_ref[owner, 2 * filts * group // share] = kept


def unpack_copied_kernel(plan, owners, chunks, in_ref, sig_hbm, fil_hbm, sig_ref, sems, fil_sem):
    _, _, group, filts = plan
    many = owners // chunks
    span = many * filts
    fil_copy = pltpu.make_async_copy(in_ref.at[:, pl.ds(filts * group, filts), :], fil_hbm, fil_sem)
    fil_copy.start()
    copies = []
    for chunk in range(chunks):
        for owner in range(chunk * many, (chunk + 1) * many):
            block = jnp.stack([in_ref[owner, pl.ds(filt * group, group), :] for filt in range(filts)], axis=0)
            for at, row in enumerate(turn_blocks(block)):
                sig_ref[at, pl.ds(owner * filts, filts), :] = row
        rows = pl.ds(chunk * span, span)
        copies.append(pltpu.make_async_copy(sig_ref.at[:, rows, :], sig_hbm.at[:, rows, :], sems.at[chunk]))
        copies[-1].start()
    for copy in copies:
        copy.wait()
    fil_copy.wait()


def pack_rows(plan, owners, cot, sig, fil):
    _, sources, group, filts = plan
    channels, local = cot.shape
    out = jax.ShapeDtypeStruct((owners, 2 * filts * group + filts, local), f32)
    if (sources, group, filts) != (2, 8, 8):
        return vmem_call(functools.partial(pack_kernel, plan, owners), out, (cot, sig, fil), "pack_rows", 1e6)
    share = filts // sources
    out = jax.ShapeDtypeStruct((owners, 2 * filts * group // share + 1, share, local), f32)
    chunks = math.gcd(owners, 4)
    grouped = (group, channels // group, local)
    return pl.pallas_call(
        functools.partial(pack_copied_kernel, plan, owners, chunks),
        out_shape=out,
        in_specs=[pl.BlockSpec(memory_space=pl.ANY)] * 3,
        out_specs=pl.BlockSpec(memory_space=pltpu.VMEM),
        scratch_shapes=[pltpu.VMEM(grouped, f32)] * 2
        + [pltpu.VMEM((owners, filts, local), f32)]
        + [pltpu.SemaphoreType.DMA((2, chunks)), pltpu.SemaphoreType.DMA],
        compiler_params=pltpu.CompilerParams(vmem_limit_bytes=44 << 20),
        cost_estimate=pl.CostEstimate(flops=0, bytes_accessed=16 * cot.size, transcendentals=0),
        name="pack_rows",
    )(*[pltpu.with_memory_space_constraint(x, pltpu.HBM) for x in (cot.reshape(grouped), sig.reshape(grouped), fil.reshape(owners, filts, local))])


def unpack_rows(plan, owners, value):
    _, _, group, filts = plan
    count, local = owners * filts, value.shape[2]
    channels = group * count
    if (group, filts) != (8, 8):
        outs = [jax.ShapeDtypeStruct((channels, local), f32), jax.ShapeDtypeStruct((count, local), f32)]
        return vmem_call(functools.partial(unpack_kernel, plan, owners), outs, (value,), "unpack_rows", 1e6)
    chunks = math.gcd(owners, 4)
    grouped = (group, count, local)
    dsig, dfil = pl.pallas_call(
        functools.partial(unpack_copied_kernel, plan, owners, chunks),
        out_shape=[jax.ShapeDtypeStruct(grouped, f32), jax.ShapeDtypeStruct((owners, filts, local), f32)],
        in_specs=[pl.BlockSpec(memory_space=pltpu.VMEM)],
        out_specs=[pl.BlockSpec(memory_space=pl.ANY)] * 2,
        scratch_shapes=[pltpu.VMEM(grouped, f32), pltpu.SemaphoreType.DMA((chunks,)), pltpu.SemaphoreType.DMA],
        compiler_params=pltpu.CompilerParams(vmem_limit_bytes=44 << 20),
        cost_estimate=pl.CostEstimate(flops=0, bytes_accessed=8 * value.size, transcendentals=0),
        name="unpack_rows",
    )(value)
    return dsig.reshape(channels, local), dfil.reshape(count, local)


def body(signal, cotangent, filters):
    ranks, halves = lax.axis_size("ctx"), lax.axis_size("tp")
    channels, local = signal.shape
    count = filters.shape[0]
    both = count % (8 * ranks * halves) == 0
    axes, sources = (("ctx", "tp"), halves) if both else ("ctx", 1)
    owners = ranks * sources
    group, filts = channels // count, count // owners
    plan = (ranks, sources, group, filts)

    def exchange(value):
        return lax.all_to_all(value, axes, split_axis=0, concat_axis=0, tiled=True)

    data = exchange(pack_rows(plan, owners, cotangent, signal, filters))
    grad_signal, grad_filters = unpack_rows(plan, owners, exchange(call_gradients(plan, data)))
    if not both:
        grad_filters = lax.psum(grad_filters, "tp")
    return grad_signal, grad_filters


def solution(mesh):
    return jax.shard_map(
        body,
        mesh=mesh,
        in_specs=(P("tp", "ctx"), P("tp", "ctx"), P(None, "ctx")),
        out_specs=(P("tp", "ctx"), P(None, "ctx")),
        check_vma=False,
    )
```
